256 devices in a mesh: group: 8 (over z_hi, x), ep: 32 (over z_lo, y, core).
Axes of the slice: x: 4, y: 4, z: 8 (z_hi: 2, z_lo: 4; z = z_hi * 4 + z_lo), core: 2. Of those that a mesh axis runs over, the one named last changes fastest.
Arguments:
- activations: bfloat16 [49152, 2560], P(('group', 'ep')), may hold values from -6 to 6
- up_grad: bfloat16 [49152, 2, 1536], P(('group', 'ep')), may hold values from -6 to 6
- gate_weights: float32 [49152, 2], P(('group', 'ep')), may hold values from 0.1 to 1
- route_slot: int32 [49152, 2], P(('group', 'ep')), may hold values from 0 to 3, all different within a row; in each aligned block of 192 rows (0 to 191, 192 to 383, ...) at most 144 rows name the same one
- placement: int32 [8, 4], replicated, may hold values from 0 to 7, as said below
- master: float32 [8, 10240, 1536], P('group', 'ep'), may hold values from -0.125 to 0.125
- moment_one: bfloat16 [8, 10240, 1536], P('group', 'ep'), may hold values from -4 to 4
- moment_two: bfloat16 [8, 10240, 1536], P('group', 'ep'), may hold values from 0.099609375 to 4
Outputs:
- input_grad: bfloat16 [49152, 2560], P(('group', 'ep'))
- master_out: float32 [8, 10240, 1536], P('group', 'ep')
- moment_one_out: bfloat16 [8, 10240, 1536], P('group', 'ep')
- moment_two_out: bfloat16 [8, 10240, 1536], P('group', 'ep')
The draws below stay inside these ranges and needn't reach their ends.
Inputs may be any that keep to these rules, and one draw needn't show every extreme that they name: `route_slot`: each token names 2 different slots; the tokens of one device name one slot at most 144 times. `placement`: slot c of every group holds an expert e with e % 4 == c; every expert is held by at least one group.
All inputs are finite; a program needn't handle non-finite values.
Results may differ from the reference program's by a relative error of at most 0.02.
Values may be sent and summed in bfloat16 or wider, within the bound.
A program may use at most 192 MiB of HBM per device.

```python
import math
import jax
import jax.numpy as jnp
import numpy as np
from jax import lax

D = 2560
H = 1536
SLOTS = 4
EXPERTS = 8
TOP = 2
TOK_DEV = 192
CAP = 144
TOKENS = 49152
N_GROUP = 8
N_EP = 32


def permute_groups(sub_key):
    return jax.random.permutation(sub_key, N_GROUP)


def draw_placement(key, part):
    key = jax.random.fold_in(key, 11)
    kind_count = EXPERTS // SLOTS
    pick_key, order_key = jax.random.split(key)
    picked = jax.random.randint(pick_key, (N_GROUP, SLOTS), 0, kind_count, dtype=jnp.int32)
    orders = jax.vmap(permute_groups)(jax.random.split(order_key, SLOTS))
    group_rank = jnp.argsort(orders, axis=1).astype(jnp.int32).T
    kind_index = jnp.where(group_rank < kind_count, group_rank, picked)
    return jnp.arange(SLOTS, dtype=jnp.int32)[None, :] + SLOTS * kind_index


def steps_of(key, extent, shards, smallest, high):
    gain, own = 1.0, jax.random.fold_in(key, 6)
    for position, shards_of in shards:
        steps = jnp.exp(jax.random.uniform(jax.random.fold_in(own, position), (shards_of,), jnp.float32, smallest / len(shards), high / len(shards)))
        gain = gain * jnp.repeat(steps, extent[position] // shards_of).reshape([-1 if axis == position else 1 for axis in range(len(extent))])
    return gain


def assign_block(stream_key, own, number, rows, number_of, top, reach, lean):
    order = jax.random.permutation(stream_key, number_of)
    heavy_load, ordinary = shares(number_of, rows * top, reach, lean, True), shares(number_of, rows * top, reach, lean, False)
    places = jnp.arange(number_of)

    def named(tallies, offset_by):
        used = int((tallies > 0).sum())
        fixed = max(1, used // 4)
        moved = fixed + (places - fixed + offset_by * (used - fixed)) % max(1, number_of - fixed)
        return jnp.zeros((number_of,), jnp.int32).at[order[jnp.where(places < fixed, places, moved)]].set(jnp.asarray(tallies, jnp.int32))

    tallies = jnp.where(number % 4 == 0, named(heavy_load, number // 4), named(ordinary, number - number // 4 - 1))
    mixed = jax.random.permutation(jax.random.fold_in(own, 3), number_of)
    source_of, sink = mixed[0:number_of // 2 * 2:2], mixed[1:number_of // 2 * 2:2]
    room = jnp.minimum(tallies[source_of] - 1, reach - tallies[sink]) // 2
    room = jnp.where((source_of == order[0]) | (sink == order[0]) | (tallies[sink] == 0), 0, jnp.maximum(room, 0))
    moved = jax.random.randint(jax.random.fold_in(own, 4), (number_of // 2,), 0, 1 << 20) % (room + 1)
    tallies = tallies.at[source_of].add(-moved).at[sink].add(moved)
    items = jnp.searchsorted(jnp.cumsum(tallies), jnp.arange(rows * top), side="right").astype(jnp.int32)
    listing = items.reshape(top, rows).T
    listing = listing[jax.random.permutation(jax.random.fold_in(own, 1), rows)]
    offset_by = jax.random.randint(jax.random.fold_in(own, 2), (rows, 1), 0, top)
    return jnp.take_along_axis(listing, (jnp.arange(top)[None, :] + offset_by) % top, axis=1)


def shares(count, total, reach, slope, full):
    loads = [(1 << 20) // math.isqrt(rank ** slope) + 1 for rank in range(1, count + 1)]
    largest = reach if full else min(reach, max(-(-total // count), total * loads[0] // sum(loads)))
    least = 1 if total - largest >= count - 1 else 0
    holding, spare = [largest] + [least] * (count - 1), total - largest - least * (count - 1)
    while spare > 0:
        candidates = [i for i in range(1, count) if holding[i] < largest] or [i for i in range(1, count) if holding[i] < reach]
        pool, left = sum([loads[i] for i in candidates]), spare
        for i in candidates:
            extra = min(reach - holding[i], max(1, left * loads[i] // pool), spare)
            holding[i] = holding[i] + extra
            spare = spare - extra
    return np.array(holding)


def normal_values(key, dims, deviation, limit, cuts=(), held_as=jnp.bfloat16):
    entries = deviation * jax.random.normal(key, dims, jnp.float32)
    if cuts:
        entries = entries * steps_of(key, dims, cuts, -0.22, 0.18)
    return jnp.clip(entries, -limit, limit).astype(held_as)


def setup_inputs(seed: int = 0) -> dict:
    keys = jax.random.split(jax.random.key(seed), 9)
    activations = normal_values(keys[0], (TOKENS, D), 1.0, 6.0, ((0, 256),))
    up_grad = normal_values(keys[1], (TOKENS, TOP, H), 1.0, 6.0, ((0, 256),))
    gate_weights = jnp.clip(0.1 + 0.9 * jax.random.uniform(keys[2], (TOKENS, TOP), jnp.float32) ** steps_of(keys[2], (TOKENS, TOP), ((0, 256),), -0.2, 0.2), 0.1, 1.0)
    route_slot_keys = jax.random.split(jax.random.fold_in(keys[3], 1), TOKENS // TOK_DEV)
    route_slot_turns = jax.random.permutation(jax.random.fold_in(keys[3], 3), TOKENS // TOK_DEV)
    route_slot = jax.vmap(lambda own, number: assign_block(jax.random.fold_in(keys[3], 2), own, number, TOK_DEV, SLOTS, TOP, CAP, 2))(route_slot_keys, route_slot_turns).reshape((TOKENS, TOP))
    placement = draw_placement(jax.random.fold_in(keys[8], 71), 0)
    master = normal_values(keys[5], (N_GROUP, SLOTS * D, H), D ** -0.5, 0.125, ((0, 8), (1, 32)), jnp.float32)
    moment_one = normal_values(keys[6], (N_GROUP, SLOTS * D, H), 0.5, 4.0, ((0, 8), (1, 32)))
    moment_two = jnp.clip(jnp.exp(math.log(4.0) - 3.6927934 * jax.random.uniform(keys[7], (N_GROUP, SLOTS * D, H), jnp.float32) ** steps_of(keys[7], (N_GROUP, SLOTS * D, H), ((0, 8), (1, 32)), -0.2, 0.2)), 0.099609375, 4.0).astype(jnp.bfloat16)
    return {"activations": activations, "up_grad": up_grad, "gate_weights": gate_weights, "route_slot": route_slot, "placement": placement, "master": master, "moment_one": moment_one, "moment_two": moment_two}


beta_one = 0.9
beta_two = 0.95
learn_rate = 0.01
decay_rate = 0.1
epsilon = 1e-08
grad_scale = 0.0625

def reference(activations, up_grad, gate_weights, route_slot, placement, master, moment_one, moment_two):
    group_rows = TOK_DEV * N_EP
    scaled = (gate_weights[:, :, None] * up_grad.astype(jnp.float32)).astype(jnp.bfloat16)

    def per_group(group_index):
        first_row = (group_index * group_rows).astype(jnp.int32)
        group_feats = lax.dynamic_slice_in_dim(activations, first_row, group_rows, 0)
        group_grads = lax.dynamic_slice_in_dim(scaled, first_row, group_rows, 0)
        group_slots = lax.dynamic_slice_in_dim(route_slot, first_row, group_rows, 0)
        weights = lax.dynamic_index_in_dim(master, group_index, 0, keepdims=False)
        accumulated = jnp.zeros((group_rows, D), jnp.float32)
        partials = []
        for slot_number in range(SLOTS):
            chosen = (group_slots == slot_number)[:, :, None]
            picked = lax.optimization_barrier(jnp.sum(jnp.where(chosen, group_grads.astype(jnp.float32), jnp.float32(0.0)), axis=1)).astype(jnp.bfloat16)
            weight_copy = weights[slot_number * D:(slot_number + 1) * D].astype(jnp.bfloat16)
            partials.append(jnp.dot(group_feats.T, picked, preferred_element_type=jnp.float32))
            slot_piece = jnp.dot(picked, weight_copy.T, preferred_element_type=jnp.float32).astype(jnp.bfloat16)
            accumulated = accumulated + slot_piece.astype(jnp.float32)
        return (accumulated.astype(jnp.bfloat16), jnp.stack(partials))
    grouped_grad, partial_value = lax.map(per_group, jnp.arange(N_GROUP, dtype=jnp.int32))
    input_grad = grouped_grad.reshape(TOKENS, D)
    same_expert = (placement[:, None, :] == placement[None, :, :]).astype(jnp.float32)
    summed = jnp.einsum('abc,bcdh->acdh', same_expert, partial_value, precision=lax.Precision.HIGHEST)
    gradient = summed.reshape(N_GROUP, SLOTS * D, H) * grad_scale
    first_moment = beta_one * moment_one.astype(jnp.float32) + (1.0 - beta_one) * gradient
    second_moment = beta_two * moment_two.astype(jnp.float32) + (1.0 - beta_two) * gradient * gradient
    update = first_moment / (1.0 - beta_one ** 10) / (jnp.sqrt(second_moment / (1.0 - beta_two ** 10)) + epsilon)
    master_out = master - learn_rate * (update + decay_rate * master)
    return (input_grad, master_out, first_moment.astype(jnp.bfloat16), second_moment.astype(jnp.bfloat16))
```

```python
import functools
from types import SimpleNamespace

import jax
import jax.numpy as jnp
from jax import lax
from jax.experimental import pallas as pl
from jax.experimental.pallas import tpu as pltpu
from jax.sharding import PartitionSpec as P

SLOTS = 4
KIND = 4

beta_one = 0.9
beta_two = 0.95
learn_rate = 0.01
decay_rate = 0.1
epsilon = 1e-08
grad_scale = 0.0625

MESH = pl.DeviceIdType.MESH
F32 = jnp.float32
BF16 = jnp.bfloat16

FULL = SimpleNamespace(ZH=2, X=4, Y=4, K=2, T=192, PW=320, NCH=6, HC=256)


def kernel(
    cfg, feat, scl, place, master, ig_out, grad_out,
    wall, fall, ft, mb, sall, pk, part, rl, rr, fin, x1r, zs, zr, x2s, g2, ba, bs, br,
    ysend, yrecv, csend, crecv, fsend, frecv, bsend, brecv,
    wrs, wrr, wls, wlr, prs, prr, pls, plr,
    x1ss, x1rs, zss, zrs, x2ss, x2rs,
):
    ZH, X, Y, K, T, PW, NCH, HC = (
        cfg.ZH, cfg.X, cfg.Y, cfg.K, cfg.T, cfg.PW, cfg.NCH, cfg.HC
    )
    E = Y * K
    LAST = SLOTS - 1
    XR = PW // X
    g, e = lax.axis_index("group"), lax.axis_index("ep")
    zh, x = g // X, g % X
    z, me = e // E, e % E
    y, k = me // K, me % K

    def plane(peer):
        return (g, z * E + peer)

    def ypeer(dy):
        return ((y + dy) % Y) * K + k

    sib = y * K + (K - 1 - k)
    left, right = (g, e - E), (g, e + E)

    def xpeer(dx):
        return (zh * X + (x + dx) % X, e)

    partner = ((ZH - 1 - zh) * X + x, e)

    def rcopy(src, dst, ss, rs, dev):
        return pltpu.make_async_remote_copy(
            src_ref=src, dst_ref=dst, send_sem=ss, recv_sem=rs, device_id=dev, device_id_type=MESH
        )

    barrier = pltpu.get_barrier_semaphore()

    def greet(dev):
        pl.semaphore_signal(barrier, inc=1, device_id=dev, device_id_type=MESH)

    for d in range(1, E):
        greet(plane((me + d) % E))
    for dx in range(1, X):
        greet(xpeer(dx))
    if ZH > 1:
        greet(partner)

    @pl.when(z > 0)
    def _():
        greet(left)

    @pl.when(z < LAST)
    def _():
        greet(right)

    pl.semaphore_wait(
        barrier,
        E - 1 + X - 1 + ZH - 1
        + jnp.where(z > 0, 1, 0) + jnp.where(z < LAST, 1, 0),
    )

    def y_copy(j, dy):
        return rcopy(scl.at[j], sall.at[j, me], ysend.at[j, dy], yrecv.at[j, dy], plane(ypeer(dy)))

    def y_from(j, dy):
        src = sall.at[j, ypeer(-dy)]
        return rcopy(src, src, ysend.at[j, dy], yrecv.at[j, dy], plane(ypeer(dy)))

    def c_copy(j, dy):
        src = scl.at[j] if dy == 0 else sall.at[j, ypeer(-dy)]
        return rcopy(src, sall.at[j, ypeer(-dy)], csend.at[j, dy], crecv.at[j, dy], plane(sib))

    def c_from(j, dy):
        src = sall.at[j, ((y - dy) % Y) * K + (K - 1 - k)]
        return rcopy(src, src, csend.at[j, dy], crecv.at[j, dy], plane(sib))

    def f_copy(d):
        peer = (me + d) % E
        return rcopy(feat.at[peer], fall.at[me], fsend.at[d], frecv.at[d], plane(peer))

    def f_from(d):
        src = fall.at[(me - d) % E]
        return rcopy(src, src, fsend.at[d], frecv.at[d], plane((me + d) % E))

    def b_copy(d):
        peer = (me + d) % E
        return rcopy(bs.at[peer], br.at[me], bsend.at[d], brecv.at[d], plane(peer))

    def b_from(d):
        src = br.at[(me - d) % E]
        return rcopy(src, src, bsend.at[d], brecv.at[d], plane((me + d) % E))

    def w_right(j, s, slot):
        return rcopy(wall.at[j, slot], wall.at[j, slot], wrs.at[j, s], wrr.at[j, s], right)

    def w_left(j, s, slot):
        return rcopy(wall.at[j, slot], wall.at[j, slot], wls.at[j, s], wlr.at[j, s], left)

    def w_from_left(j, s, slot):
        return rcopy(wall.at[j, slot], wall.at[j, slot], wrs.at[j, s], wrr.at[j, s], left)

    def w_from_right(j, s, slot):
        return rcopy(wall.at[j, slot], wall.at[j, slot], wls.at[j, s], wlr.at[j, s], right)

    def p_right(j, c):
        return rcopy(part.at[j, c], rl.at[j, c - 1], prs.at[j, c], prr.at[j, c], right)

    def p_left(j, c):
        return rcopy(part.at[j, c], rr.at[j, c], pls.at[j, c], plr.at[j, c], left)

    def p_from_left(j, c):
        return rcopy(rl.at[j, c - 1], rl.at[j, c - 1], prs.at[j, c], prr.at[j, c], left)

    def p_from_right(j, c):
        return rcopy(rr.at[j, c], rr.at[j, c], pls.at[j, c], plr.at[j, c], right)

    def xrows(who):
        return pl.ds(pl.multiple_of(who * XR, 16), XR)

    def x1_copy(j, dx):
        return rcopy(
            fin.at[j, xrows((x + dx) % X)], x1r.at[j, x], x1ss.at[j, dx], x1rs.at[j, dx], xpeer(dx)
        )

    def x1_from(j, dx):
        src = x1r.at[j, (x - dx) % X]
        return rcopy(src, src, x1ss.at[j, dx], x1rs.at[j, dx], xpeer(dx))

    def z_copy(j):
        return rcopy(zs.at[j], zr.at[j], zss.at[j], zrs.at[j], partner)

    def x2_copy(j, dx):
        return rcopy(
            x2s.at[j, dx], g2.at[j, xrows(x)], x2ss.at[j, dx], x2rs.at[j, dx], xpeer(dx)
        )

    def x2_from(j, dx):
        src = g2.at[j, xrows((x - dx) % X)]
        return rcopy(src, src, x2ss.at[j, dx], x2rs.at[j, dx], xpeer(dx))

    def send_scaled(j):
        for dy in range(1, Y):
            y_copy(j, dy).start()
        if K > 1:
            c_copy(j, 0).start()

    def send_weights(j):
        @pl.when(z < LAST)
        def _():
            w_right(j, 0, z).start()

        @pl.when(z > 0)
        def _():
            w_left(j, 0, z).start()

    def pass_weights(j, s):
        zm = LAST - z

        @pl.when(z >= s)
        def _():
            w_from_left(j, s - 1, z - s).wait_recv()

        @pl.when((z >= s) & (z < LAST))
        def _():
            w_right(j, s, z - s).start()

        @pl.when(zm >= s)
        def _():
            w_from_right(j, s - 1, z + s).wait_recv()

        @pl.when((zm >= s) & (z > 0))
        def _():
            w_left(j, s, z + s).start()

    def partials(j, ring):
        def pick(b, _):
            for c in range(SLOTS):
                m0 = mb[b, :, (2 * c) * 128:(2 * c + 1) * 128]
                m1 = mb[b, :, (2 * c + 1) * 128:(2 * c + 2) * 128]
                for l in range(HC // 128):
                    cols = slice(l * 128, (l + 1) * 128)
                    pk[ring, c, b, :, cols] = (
                        sall[j, b, 0, :, cols] * m0 + sall[j, b, 1, :, cols] * m1
                    )
            return 0

        lax.fori_loop(0, E, pick, 0)

        def one(c, _):
            part[j, c] = jnp.dot(
                ft[...], pk[ring, c].reshape(E * T, HC), preferred_element_type=F32
            ).astype(BF16)
            return 0

        lax.fori_loop(0, SLOTS, one, 0)

    def reduce_stage(j, s):
        @pl.when(z == s)
        def _():
            for c in range(LAST, s, -1):
                if s > 0:
                    p_from_left(j, c).wait_recv()
                    part[j, c] = (part[j, c].astype(F32) + rl[j, c - 1].astype(F32)).astype(BF16)
                p_right(j, c).start()

        @pl.when(z == LAST - s)
        def _():
            for c in range(0, LAST - s):
                if s > 0:
                    p_from_right(j, c).wait_recv()
                    part[j, c] = (part[j, c].astype(F32) + rr[j, c].astype(F32)).astype(BF16)
                p_left(j, c).start()

    def finish(j):
        for zz in range(SLOTS):
            @pl.when(z == zz)
            def _(zz=zz):
                total = part[j, zz].astype(F32)
                if zz > 0:
                    p_from_left(j, zz).wait_recv()
                    total = total + rl[j, zz - 1].astype(F32)
                if zz < LAST:
                    p_from_right(j, zz).wait_recv()
                    total = total + rr[j, zz].astype(F32)
                fin[j] = total.astype(BF16)

        for dx in range(1, X):
            x1_copy(j, dx).start()

    def kind_of(who):
        return jnp.where(place[zh * X + who, z] >= KIND, 1.0, 0.0).astype(F32)

    def kind_sums(j):
        own = fin[j, xrows(x)].astype(F32)
        weight = kind_of(x)
        one = own * weight
        zero = own * (1.0 - weight)
        for dx in range(1, X):
            x1_from(j, dx).wait_recv()
            who = (x - dx) % X
            weight = kind_of(who)
            got = x1r[j, who].astype(F32)
            one += got * weight
            zero += got * (1.0 - weight)
        zs[j, 0] = zero.astype(BF16)
        zs[j, 1] = one.astype(BF16)
        if ZH > 1:
            z_copy(j).start()

    def spread(j):
        zero, one = zs[j, 0].astype(F32), zs[j, 1].astype(F32)
        if ZH > 1:
            z_copy(j).wait_recv()
            zero += zr[j, 0].astype(F32)
            one += zr[j, 1].astype(F32)
        for dx in range(X):
            weight = kind_of((x + dx) % X)
            chosen = (one * weight + zero * (1.0 - weight)).astype(BF16)
            if dx == 0:
                g2[j, xrows(x)] = chosen
            else:
                x2s[j, dx] = chosen
                x2_copy(j, dx).start()

    def collect(j):
        for dx in range(1, X):
            x2_from(j, dx).wait_recv()
        grad_out[:, pl.ds(pl.multiple_of(j * HC, HC), HC)] = g2[j]

    def back(j, ring):
        def block(b, _):
            total = ba[b]
            for c in range(SLOTS):
                total += lax.dot_general(
                    pk[ring, c, b], wall[j, c], (((1,), (1,)), ((), ())),
                    preferred_element_type=F32,
                )
            ba[b] = total
            return 0

        lax.fori_loop(0, E, block, 0)

    for j in range(NCH):
        wall[j, z] = master[:, j * HC:(j + 1) * HC].astype(BF16)
        if j < 3:
            send_weights(j)
        if j == 0:
            for d in range(1, E):
                f_copy(d).start()
        if j < 2:
            send_scaled(j)

    def own_rows(j, _):
        sall[j, me] = scl[j]
        return 0

    lax.fori_loop(0, NCH, own_rows, 0)
    fall[me] = feat[me]

    def clear(b, _):
        ba[b] = jnp.zeros((T, PW), F32)
        return 0

    lax.fori_loop(0, E, clear, 0)

    for d in range(1, E):
        f_from(d).wait_recv()

    first = (PW // 128) * 128
    spot = lax.broadcasted_iota(jnp.int32, (128, 2 * SLOTS * 128), 0)
    lane = lax.broadcasted_iota(jnp.int32, (128, 2 * SLOTS * 128), 1)
    pick_lane = jnp.where(spot - (PW - first) == lane // 128, 1.0, 0.0).astype(BF16)

    def masks(b, _):
        mb[b] = jnp.dot(
            fall[b, :, first:first + 128], pick_lane, preferred_element_type=F32
        ).astype(BF16)
        return 0

    lax.fori_loop(0, E, masks, 0)
    ft[...] = fall[...].reshape(E * T, fall.shape[2]).T[:PW]

    def when_chunk(i, lag, f):
        j = i - lag

        @pl.when((j >= 0) & (j < NCH))
        def _():
            f(j)

    def step(i, _):
        def gather(j):
            for dy in range(1, Y):
                y_from(j, dy).wait_recv()
                if K > 1:
                    c_copy(j, dy).start()

        when_chunk(i, 0, gather)
        when_chunk(i, -2, send_scaled)
        when_chunk(i, 0, lambda j: pass_weights(j, 1))
        when_chunk(i, 1, lambda j: pass_weights(j, 2))
        when_chunk(i, 2, lambda j: pass_weights(j, 3))
        when_chunk(i, -3, send_weights)

        def compute(j):
            if K > 1:
                for dy in range(Y):
                    c_from(j, dy).wait_recv()
            partials(j, j % 3)
            reduce_stage(j, 0)

        when_chunk(i, 0, compute)
        when_chunk(i, 1, lambda j: reduce_stage(j, 1))
        when_chunk(i, 2, lambda j: reduce_stage(j, 2))
        when_chunk(i, 3, finish)
        when_chunk(i, 4, kind_sums)
        when_chunk(i, 5, spread)
        when_chunk(i, 6, collect)
        when_chunk(i, 2, lambda j: back(j, j % 3))

        @pl.when(i == NCH + 1)
        def _():
            def out(b, _):
                bs[b] = ba[b].astype(BF16)
                return 0

            lax.fori_loop(0, E, out, 0)
            for d in range(1, E):
                b_copy(d).start()

        return 0

    lax.fori_loop(0, NCH + 7, step, 0)

    br[me] = bs[me]
    for d in range(1, E):
        b_from(d).wait_recv()
    ig_out[...] = br[...]

    for d in range(1, E):
        f_copy(d).wait_send()
        b_copy(d).wait_send()

    def drain(j, _):
        for dy in range(1, Y):
            y_copy(j, dy).wait_send()
        if K > 1:
            for dy in range(Y):
                c_copy(j, dy).wait_send()
        for s in range(SLOTS - 1):
            @pl.when((z >= s) & (z < LAST))
            def _(s=s):
                w_right(j, s, z - s).wait_send()

            @pl.when((LAST - z >= s) & (z > 0))
            def _(s=s):
                w_left(j, s, z + s).wait_send()

            @pl.when(z == s)
            def _(s=s):
                for c in range(LAST, s, -1):
                    p_right(j, c).wait_send()

            @pl.when(z == LAST - s)
            def _(s=s):
                for c in range(0, LAST - s):
                    p_left(j, c).wait_send()

        for dx in range(1, X):
            x1_copy(j, dx).wait_send()
            x2_copy(j, dx).wait_send()
        if ZH > 1:
            z_copy(j).wait_send()
        return 0

    lax.fori_loop(0, NCH, drain, 0)


def exchange(cfg, feat, scl, place, master):
    ZH, X, Y, K, T, PW, NCH, HC = (
        cfg.ZH, cfg.X, cfg.Y, cfg.K, cfg.T, cfg.PW, cfg.NCH, cfg.HC
    )
    E = Y * K
    PWL = feat.shape[2]
    XR = PW // X
    DMA = pltpu.SemaphoreType.DMA
    vm = pl.BlockSpec(memory_space=pltpu.VMEM)
    sm = pl.BlockSpec(memory_space=pltpu.SMEM)

    def sems(*shape):
        return [DMA(shape), DMA(shape)]

    return pl.pallas_call(
        functools.partial(kernel, cfg),
        out_shape=(
            jax.ShapeDtypeStruct((E, T, PW), BF16),
            jax.ShapeDtypeStruct((PW, NCH * HC), BF16),
        ),
        in_specs=[vm, vm, sm, vm],
        out_specs=(vm, vm),
        scratch_shapes=[
            pltpu.VMEM((NCH, SLOTS, PW, HC), BF16),
            pltpu.VMEM((E, T, PWL), BF16),
            pltpu.VMEM((PW, E * T), BF16),
            pltpu.VMEM((E, T, 2 * SLOTS * 128), BF16),
            pltpu.VMEM((NCH, E, 2, T, HC), BF16),
            pltpu.VMEM((3, SLOTS, E, T, HC), BF16),
            pltpu.VMEM((NCH, SLOTS, PW, HC), BF16),
            pltpu.VMEM((NCH, SLOTS - 1, PW, HC), BF16),
            pltpu.VMEM((NCH, SLOTS - 1, PW, HC), BF16),
            pltpu.VMEM((NCH, PW, HC), BF16),
            pltpu.VMEM((NCH, X, XR, HC), BF16),
            pltpu.VMEM((NCH, 2, XR, HC), BF16),
            pltpu.VMEM((NCH, 2, XR, HC), BF16),
            pltpu.VMEM((NCH, X, XR, HC), BF16),
            pltpu.VMEM((NCH, PW, HC), BF16),
            pltpu.VMEM((E, T, PW), F32),
            pltpu.VMEM((E, T, PW), BF16),
            pltpu.VMEM((E, T, PW), BF16),
            *sems(NCH, Y), *sems(NCH, Y), *sems(E), *sems(E),
            *sems(NCH, SLOTS), *sems(NCH, SLOTS), *sems(NCH, SLOTS), *sems(NCH, SLOTS),
            *sems(NCH, X), *sems(NCH), *sems(NCH, X),
        ],
        compiler_params=pltpu.CompilerParams(
            collective_id=0, has_side_effects=True, vmem_limit_bytes=62 << 20
        ),
        name="exchange",
    )(feat, scl, place, master)


def on_device(
    cfg, activations, up_grad, gate_weights, route_slot, placement, master, moment_one, moment_two
):
    E, T, PW, NCH, HC = cfg.Y * cfg.K, cfg.T, cfg.PW, cfg.NCH, cfg.HC
    scaled = (gate_weights[:, :, None] * up_grad.astype(F32)).astype(BF16)
    scl = scaled.reshape(T, 2, NCH, HC).transpose(2, 1, 0, 3)
    pad = -PW % 128
    onehot = (
        route_slot[:, None, :] == jnp.arange(SLOTS, dtype=jnp.int32)[None, :, None]
    ).reshape(T, 2 * SLOTS).astype(BF16)
    marks = jnp.pad(onehot, ((0, 0), (0, pad - 2 * SLOTS)))
    feat = jnp.concatenate(
        [
            activations.reshape(T, E, PW).transpose(1, 0, 2),
            jnp.broadcast_to(marks[None], (E, T, pad)),
        ],
        axis=2,
    )
    back, grad = exchange(cfg, feat, scl, placement, master[0])
    input_grad = back.transpose(1, 0, 2).reshape(T, E * PW)
    gradient = grad.astype(F32) * grad_scale
    first_moment = beta_one * moment_one[0].astype(F32) + (1.0 - beta_one) * gradient
    second_moment = (
        beta_two * moment_two[0].astype(F32) + (1.0 - beta_two) * gradient * gradient
    )
    update = (
        first_moment
        / (1.0 - beta_one**10)
        / (jnp.sqrt(second_moment / (1.0 - beta_two**10)) + epsilon)
    )
    master_out = master[0] - learn_rate * (update + decay_rate * master[0])
    return (
        input_grad,
        master_out[None],
        first_moment.astype(BF16)[None],
        second_moment.astype(BF16)[None],
    )


def solution(mesh, cfg=FULL):
    in_specs = (
        P(("group", "ep"), None),
        P(("group", "ep"), None, None),
        P(("group", "ep"), None),
        P(("group", "ep"), None),
        P(),
        P("group", "ep", None),
        P("group", "ep", None),
        P("group", "ep", None),
    )
    out_specs = (
        P(("group", "ep"), None),
        P("group", "ep", None),
        P("group", "ep", None),
        P("group", "ep", None),
    )
    return jax.shard_map(
        functools.partial(on_device, cfg),
        mesh=mesh, in_specs=in_specs, out_specs=out_specs, check_vma=False,
    )
```

```python
import functools
from types import SimpleNamespace

import jax
import jax.numpy as jnp
from jax import lax
from jax.experimental import pallas as pl
from jax.experimental.pallas import tpu as pltpu
from jax.sharding import PartitionSpec as P

SLOTS = 4
KIND = 4

beta_one = 0.9
beta_two = 0.95
learn_rate = 0.01
decay_rate = 0.1
epsilon = 1e-08
grad_scale = 0.0625

MESH = pl.DeviceIdType.MESH
F32 = jnp.float32
BF16 = jnp.bfloat16

FULL = SimpleNamespace(ZH=2, X=4, Y=4, K=2, T=192, PW=320, NCH=6, HC=256, RING=3, BACK=2)


def kernel(
    cfg, feat, grads, gates, slots, place, master, mom1, mom2,
    ig_out, master_out, mom1_out, mom2_out,
    fv, uv, mv, v1, v2, gm, fs,
    wall, fall, ft, mb, sall, pk, part, ks, rl, rr, x1r, zs, zr, x2s, g2, ba, bs, br,
    ysend, yrecv, hsend, hrecv, csend, crecv, osend, orecv, fsend, frecv, bsend, brecv,
    wrs, wrr, wls, wlr, prs, prr, pls, plr,
    x1ss, x1rs, zss, zrs, x2ss, x2rs,
    lsem, msem, v1sem, v2sem, mosem, o1sem, o2sem,
):
    ZH, X, Y, K, T, PW, NCH, HC = (
        cfg.ZH, cfg.X, cfg.Y, cfg.K, cfg.T, cfg.PW, cfg.NCH, cfg.HC
    )
    E = Y * K
    LAST = SLOTS - 1
    XR = PW // X
    near = {1: (), 2: (1,), 4: (1, 3)}[Y]
    RING, BACK = cfg.RING, cfg.BACK
    g, e = lax.axis_index("group"), lax.axis_index("ep")
    zh, x = g // X, g % X
    z, me = e // E, e % E
    y, k = me // K, me % K

    def plane(peer):
        return (g, z * E + peer)

    def ypeer(dy):
        return ((y + dy) % Y) * K + k

    sib = y * K + (K - 1 - k)
    left, right = (g, e - E), (g, e + E)

    def xpeer(dx):
        return (zh * X + (x + dx) % X, e)

    partner = ((ZH - 1 - zh) * X + x, e)

    def rcopy(src, dst, ss, rs, dev):
        return pltpu.make_async_remote_copy(
            src_ref=src, dst_ref=dst, send_sem=ss, recv_sem=rs, device_id=dev, device_id_type=MESH
        )

    def cols(j):
        return pl.ds(pl.multiple_of(j * HC, HC), HC)

    def load_master(j):
        return pltpu.make_async_copy(master.at[:, cols(j)], mv.at[j], msem.at[j])

    def load_mom1(j):
        return pltpu.make_async_copy(mom1.at[:, cols(j)], v1.at[j], v1sem.at[j])

    def load_mom2(j):
        return pltpu.make_async_copy(mom2.at[:, cols(j)], v2.at[j], v2sem.at[j])

    def store_master(j):
        return pltpu.make_async_copy(mv.at[j], master_out.at[:, cols(j)], mosem.at[j])

    def store_mom1(j):
        return pltpu.make_async_copy(v1.at[j], mom1_out.at[:, cols(j)], o1sem.at[j])

    def store_mom2(j):
        return pltpu.make_async_copy(v2.at[j], mom2_out.at[:, cols(j)], o2sem.at[j])

    load_feat = pltpu.make_async_copy(feat, fv, lsem.at[0])
    load_grads = pltpu.make_async_copy(grads, uv, lsem.at[1])
    load_feat.start()
    load_grads.start()
    for j in range(NCH):
        load_master(j).start()

    barrier = pltpu.get_barrier_semaphore()

    def greet(dev):
        pl.semaphore_signal(barrier, inc=1, device_id=dev, device_id_type=MESH)

    for d in range(1, E):
        greet(plane((me + d) % E))
    for dx in range(1, X):
        greet(xpeer(dx))
    if ZH > 1:
        greet(partner)

    @pl.when(z > 0)
    def _():
        greet(left)

    @pl.when(z < LAST)
    def _():
        greet(right)

    marks = [
        jnp.where(slots[r:r + 1, :] == c, 1.0, 0.0) for c in range(SLOTS) for r in range(2)
    ]
    marks = jnp.concatenate(
        marks + [gates[...], jnp.zeros((128 - 2 * SLOTS - 2, T), F32)], axis=0
    )
    wide = -T % 128
    if wide:
        marks = jnp.concatenate([marks, jnp.zeros((128, wide), F32)], axis=1)
    gm[...] = marks.T[:T]

    PWL = fs.shape[2]
    tail = gm[:, :PWL - PW].astype(BF16)
    load_feat.wait()
    for d in range(E):
        fs[d] = jnp.concatenate([fv[:, d * PW:(d + 1) * PW], tail], axis=1)

    def scale(j):
        for r in range(2):
            gate = gm[:, 2 * SLOTS + r:2 * SLOTS + r + 1]
            sall[j, me, r] = (uv[:, r, cols(j)].astype(F32) * gate).astype(BF16)

    def weights(j):
        load_master(j).wait()
        wall[j, z] = mv[j].astype(BF16)

    load_grads.wait()
    scale(0)
    weights(0)

    pl.semaphore_wait(
        barrier,
        E - 1 + X - 1 + ZH - 1
        + jnp.where(z > 0, 1, 0) + jnp.where(z < LAST, 1, 0),
    )

    def y_copy(j, dy):
        return rcopy(sall.at[j, me], sall.at[j, me], ysend.at[j, dy], yrecv.at[j, dy], plane(ypeer(dy)))

    def y_from(j, dy):
        src = sall.at[j, ypeer(-dy)]
        return rcopy(src, src, ysend.at[j, dy], yrecv.at[j, dy], plane(ypeer(dy)))

    def c_copy(j, dy):
        src = sall.at[j, ypeer(-dy)]
        return rcopy(src, src, csend.at[j, dy], crecv.at[j, dy], plane(sib))

    def c_from(j, dy):
        src = sall.at[j, ((y - dy) % Y) * K + (K - 1 - k)]
        return rcopy(src, src, csend.at[j, dy], crecv.at[j, dy], plane(sib))

    def h_copy(j, dy):
        h = 0 if dy == 1 else 1
        src = sall.at[j, ypeer(-dy), h]
        return rcopy(src, src, hsend.at[j, h], hrecv.at[j, h], plane(ypeer(dy)))

    def h_from(j, h):
        src = sall.at[j, ypeer(2), h]
        return rcopy(src, src, hsend.at[j, h], hrecv.at[j, h], plane(ypeer(1)))

    def o_copy(j, h):
        src = sall.at[j, ypeer(2), h]
        return rcopy(src, src, osend.at[j, h], orecv.at[j, h], plane(sib))

    def o_from(j, h):
        src = sall.at[j, ((y + 2) % Y) * K + (K - 1 - k), h]
        return rcopy(src, src, osend.at[j, h], orecv.at[j, h], plane(sib))

    def f_copy(d):
        peer = (me + d) % E
        return rcopy(fs.at[peer], fall.at[me], fsend.at[d], frecv.at[d], plane(peer))

    def f_from(d):
        src = fall.at[(me - d) % E]
        return rcopy(src, src, fsend.at[d], frecv.at[d], plane((me + d) % E))

    def b_copy(d):
        peer = (me + d) % E
        return rcopy(bs.at[peer], br.at[me], bsend.at[d], brecv.at[d], plane(peer))

    def b_from(d):
        src = br.at[(me - d) % E]
        return rcopy(src, src, bsend.at[d], brecv.at[d], plane((me + d) % E))

    def w_right(j, s, slot):
        return rcopy(wall.at[j, slot], wall.at[j, slot], wrs.at[j, s], wrr.at[j, s], right)

    def w_left(j, s, slot):
        return rcopy(wall.at[j, slot], wall.at[j, slot], wls.at[j, s], wlr.at[j, s], left)

    def w_from_left(j, s, slot):
        return rcopy(wall.at[j, slot], wall.at[j, slot], wrs.at[j, s], wrr.at[j, s], left)

    def w_from_right(j, s, slot):
        return rcopy(wall.at[j, slot], wall.at[j, slot], wls.at[j, s], wlr.at[j, s], right)

    def p_right(j, c):
        return rcopy(ks.at[j, c], rl.at[j, c - 1], prs.at[j, c], prr.at[j, c], right)

    def p_left(j, c):
        return rcopy(ks.at[j, c], rr.at[j, c], pls.at[j, c], plr.at[j, c], left)

    def p_from_left(j, c):
        return rcopy(rl.at[j, c - 1], rl.at[j, c - 1], prs.at[j, c], prr.at[j, c], left)

    def p_from_right(j, c):
        return rcopy(rr.at[j, c], rr.at[j, c], pls.at[j, c], plr.at[j, c], right)

    def xrows(who):
        return pl.ds(pl.multiple_of(who * XR, 16), XR)

    def x1_copy(j, dx):
        return rcopy(
            part.at[j, :, xrows((x + dx) % X)], x1r.at[j, x],
            x1ss.at[j, dx], x1rs.at[j, dx], xpeer(dx),
        )

    def x1_from(j, dx):
        src = x1r.at[j, (x - dx) % X]
        return rcopy(src, src, x1ss.at[j, dx], x1rs.at[j, dx], xpeer(dx))

    def z_copy(j):
        return rcopy(zs.at[j], zr.at[j], zss.at[j], zrs.at[j], partner)

    def x2_copy(j, dx):
        return rcopy(
            x2s.at[j, dx], g2.at[j, xrows(x)], x2ss.at[j, dx], x2rs.at[j, dx], xpeer(dx)
        )

    def x2_from(j, dx):
        src = g2.at[j, xrows((x - dx) % X)]
        return rcopy(src, src, x2ss.at[j, dx], x2rs.at[j, dx], xpeer(dx))

    def send_scaled(j):
        for dy in near:
            y_copy(j, dy).start()
        if K > 1:
            c_copy(j, 0).start()

    def send_weights(j):
        @pl.when(z < LAST)
        def _():
            w_right(j, 0, z).start()

        @pl.when(z > 0)
        def _():
            w_left(j, 0, z).start()

    def pass_weights(j, s):
        zm = LAST - z

        @pl.when(z >= s)
        def _():
            w_from_left(j, s - 1, z - s).wait_recv()

        @pl.when((z >= s) & (z < LAST))
        def _():
            w_right(j, s, z - s).start()

        @pl.when(zm >= s)
        def _():
            w_from_right(j, s - 1, z + s).wait_recv()

        @pl.when((zm >= s) & (z > 0))
        def _():
            w_left(j, s, z + s).start()

    def when_chunk(i, lag, f):
        j = i - lag

        @pl.when((j >= 0) & (j < NCH))
        def _():
            f(j)

    def gather_near(j):
        for dy in near:
            y_from(j, dy).wait_recv()
            if Y == 4:
                h_copy(j, dy).start()
            if K > 1:
                c_copy(j, dy).start()

    def gather_far(j):
        if Y == 4:
            for h in range(2):
                h_from(j, h).wait_recv()
                if K > 1:
                    o_copy(j, h).start()

    def partials(j, ring):
        def pick(b, _):
            for c in range(SLOTS):
                m0 = mb[b, :, (2 * c) * 128:(2 * c + 1) * 128]
                m1 = mb[b, :, (2 * c + 1) * 128:(2 * c + 2) * 128]
                for l in range(HC // 128):
                    ln = slice(l * 128, (l + 1) * 128)
                    pk[ring, c, b, :, ln] = (
                        sall[j, b, 0, :, ln] * m0 + sall[j, b, 1, :, ln] * m1
                    )
            return 0

        lax.fori_loop(0, E, pick, 0)

        def one(c, _):
            part[j, c] = jnp.dot(
                ft[...], pk[ring, c].reshape(E * T, HC), preferred_element_type=F32
            ).astype(BF16)
            return 0

        lax.fori_loop(0, SLOTS, one, 0)

    def kind_of(who, c):
        return jnp.where(place[c, zh * X + who] >= KIND, 1.0, 0.0).astype(F32)

    def kind_sums(j):
        for dx in range(1, X):
            x1_from(j, dx).wait_recv()

        def one(c, _):
            own = part[j, c, xrows(x)].astype(F32)
            weight = kind_of(x, c)
            second = own * weight
            total = own
            for dx in range(1, X):
                who = (x - dx) % X
                got = x1r[j, who, c].astype(F32)
                second += got * kind_of(who, c)
                total += got
            ks[j, c, 0] = (total - second).astype(BF16)
            ks[j, c, 1] = second.astype(BF16)
            return 0

        lax.fori_loop(0, SLOTS, one, 0)

    def reduce_stage(j, s):
        @pl.when(z == s)
        def _():
            for c in range(LAST, s, -1):
                if s > 0:
                    p_from_left(j, c).wait_recv()
                    ks[j, c] = (ks[j, c].astype(F32) + rl[j, c - 1].astype(F32)).astype(BF16)
                p_right(j, c).start()

        @pl.when(z == LAST - s)
        def _():
            for c in range(0, LAST - s):
                if s > 0:
                    p_from_right(j, c).wait_recv()
                    ks[j, c] = (ks[j, c].astype(F32) + rr[j, c].astype(F32)).astype(BF16)
                p_left(j, c).start()

    def finish(j):
        for zz in range(SLOTS):
            @pl.when(z == zz)
            def _(zz=zz):
                total = ks[j, zz].astype(F32)
                if zz > 0:
                    p_from_left(j, zz).wait_recv()
                    total = total + rl[j, zz - 1].astype(F32)
                if zz < LAST:
                    p_from_right(j, zz).wait_recv()
                    total = total + rr[j, zz].astype(F32)
                zs[j] = total.astype(BF16)

        if ZH > 1:
            z_copy(j).start()

    def spread(j):
        zero, one = zs[j, 0].astype(F32), zs[j, 1].astype(F32)
        if ZH > 1:
            z_copy(j).wait_recv()
            zero += zr[j, 0].astype(F32)
            one += zr[j, 1].astype(F32)
        for dx in range(X):
            weight = kind_of((x + dx) % X, z)
            chosen = (one * weight + zero * (1.0 - weight)).astype(BF16)
            if dx == 0:
                g2[j, xrows(x)] = chosen
            else:
                x2s[j, dx] = chosen
                x2_copy(j, dx).start()

    def collect(j):
        for dx in range(1, X):
            x2_from(j, dx).wait_recv()
        load_mom1(j).wait()
        load_mom2(j).wait()

        def update(b, _):
            rows = xrows(b)
            gradient = g2[j, rows].astype(F32) * grad_scale
            first = beta_one * v1[j, rows].astype(F32) + (1.0 - beta_one) * gradient
            second = beta_two * v2[j, rows].astype(F32) + (1.0 - beta_two) * gradient * gradient
            change = (
                first
                / (1.0 - beta_one**10)
                / (jnp.sqrt(second / (1.0 - beta_two**10)) + epsilon)
            )
            old = mv[j, rows]
            mv[j, rows] = old - learn_rate * (change + decay_rate * old)
            v1[j, rows] = first.astype(BF16)
            v2[j, rows] = second.astype(BF16)
            return 0

        lax.fori_loop(0, X, update, 0)
        store_master(j).start()
        store_mom1(j).start()
        store_mom2(j).start()

    def back(j, ring):
        pass_weights(j, 3)

        def block(b, _):
            total = ba[b]
            for c in range(SLOTS):
                total += lax.dot_general(
                    pk[ring, c, b], wall[j, c], (((1,), (1,)), ((), ())),
                    preferred_element_type=F32,
                )
            ba[b] = total
            return 0

        lax.fori_loop(0, E, block, 0)

    for d in range(1, E):
        f_copy(d).start()
    send_scaled(0)
    send_weights(0)

    def prepare(j, _):
        scale(j)
        weights(j)

        send_weights(j)
        load_mom1(j).start()
        load_mom2(j).start()
        return 0

    load_mom1(0).start()
    load_mom2(0).start()
    lax.fori_loop(1, NCH, prepare, 0)
    fall[me] = fs[me]

    def clear(b, _):
        ba[b] = jnp.zeros((T, PW), F32)
        return 0

    lax.fori_loop(0, E, clear, 0)

    for j in range(NCH // 2):
        pass_weights(j, 1)
    gather_near(0)
    send_scaled(1)
    gather_far(0)
    for j in range(NCH // 2, NCH):
        pass_weights(j, 1)
    for d in range(1, E):
        f_from(d).wait_recv()

    first = (PW // 128) * 128
    spot = lax.broadcasted_iota(jnp.int32, (128, 2 * SLOTS * 128), 0)
    lane = lax.broadcasted_iota(jnp.int32, (128, 2 * SLOTS * 128), 1)
    pick_lane = jnp.where(spot - (PW - first) == lane // 128, 1.0, 0.0).astype(BF16)

    def masks(b, _):
        mb[b] = jnp.dot(
            fall[b, :, first:first + 128], pick_lane, preferred_element_type=F32
        ).astype(BF16)
        return 0

    lax.fori_loop(0, E, masks, 0)
    ft[...] = fall[...].reshape(E * T, fall.shape[2]).T[:PW]

    def step(i, _):
        when_chunk(i, -2, send_scaled)
        when_chunk(i, -1, gather_near)
        when_chunk(2 * i, 0, lambda j: pass_weights(j, 2))
        when_chunk(2 * i + 1, 0, lambda j: pass_weights(j, 2))

        def sums(j):
            kind_sums(j)
            reduce_stage(j, 0)


        def compute(j):
            if K > 1:
                for dy in (0, *near):
                    c_from(j, dy).wait_recv()
                if Y == 4:
                    for h in range(2):
                        o_from(j, h).wait_recv()
            partials(j, j % RING)
            for dx in range(1, X):
                x1_copy(j, dx).start()

        when_chunk(i, 0, compute)
        when_chunk(i, -1, gather_far)
        when_chunk(i, 1, sums)
        when_chunk(i, 2, lambda j: reduce_stage(j, 1))
        when_chunk(i, 3, lambda j: reduce_stage(j, 2))
        when_chunk(i, 4, finish)
        when_chunk(i, 5, spread)
        when_chunk(i, 6, collect)
        when_chunk(i, BACK, lambda j: back(j, j % RING))

        @pl.when(i == NCH - 1 + BACK)
        def _():
            def out(b, _):
                bs[b, :, :PW] = ba[b].astype(BF16)
                return 0

            lax.fori_loop(0, E, out, 0)
            for d in range(1, E):
                b_copy(d).start()

        return 0

    lax.fori_loop(0, NCH + 7, step, 0)

    br[me] = bs[me]
    for d in range(1, E):
        b_from(d).wait_recv()
    for d in range(E):
        ig_out[:, d * PW:(d + 1) * PW] = br[d, :, :PW]

    for d in range(1, E):
        f_copy(d).wait_send()
        b_copy(d).wait_send()

    def drain(j, _):
        for dy in near:
            y_copy(j, dy).wait_send()
            if Y == 4:
                h_copy(j, dy).wait_send()
        if K > 1:
            for dy in (0, *near):
                c_copy(j, dy).wait_send()
            if Y == 4:
                for h in range(2):
                    o_copy(j, h).wait_send()
        for s in range(SLOTS - 1):
            @pl.when((z >= s) & (z < LAST))
            def _(s=s):
                w_right(j, s, z - s).wait_send()

            @pl.when((LAST - z >= s) & (z > 0))
            def _(s=s):
                w_left(j, s, z + s).wait_send()

            @pl.when(z == s)
            def _(s=s):
                for c in range(LAST, s, -1):
                    p_right(j, c).wait_send()

            @pl.when(z == LAST - s)
            def _(s=s):
                for c in range(0, LAST - s):
                    p_left(j, c).wait_send()

        for dx in range(1, X):
            x1_copy(j, dx).wait_send()
            x2_copy(j, dx).wait_send()
        if ZH > 1:
            z_copy(j).wait_send()
        store_master(j).wait()
        store_mom1(j).wait()
        store_mom2(j).wait()
        return 0

    lax.fori_loop(0, NCH, drain, 0)


def on_device(
    cfg, activations, up_grad, gate_weights, route_slot, placement, master, moment_one, moment_two
):
    X, Y, K, T, PW, NCH, HC = cfg.X, cfg.Y, cfg.K, cfg.T, cfg.PW, cfg.NCH, cfg.HC
    E = Y * K
    PWL = PW + -PW % 128
    XR = PW // X
    DMA = pltpu.SemaphoreType.DMA
    vm = pl.BlockSpec(memory_space=pltpu.VMEM)
    sm = pl.BlockSpec(memory_space=pltpu.SMEM)
    hbm = pl.BlockSpec(memory_space=pl.ANY)

    def sems(*shape):
        return [DMA(shape), DMA(shape)]

    outs = pl.pallas_call(
        functools.partial(kernel, cfg),
        out_shape=(
            jax.ShapeDtypeStruct((T, E * PW), BF16),
            jax.ShapeDtypeStruct((PW, NCH * HC), F32),
            jax.ShapeDtypeStruct((PW, NCH * HC), BF16),
            jax.ShapeDtypeStruct((PW, NCH * HC), BF16),
        ),
        in_specs=[hbm, hbm, vm, vm, sm, hbm, hbm, hbm],
        out_specs=(vm, hbm, hbm, hbm),
        scratch_shapes=[
            pltpu.VMEM((T, E * PW), BF16),
            pltpu.VMEM((T, 2, NCH * HC), BF16),
            pltpu.VMEM((NCH, PW, HC), F32),
            pltpu.VMEM((NCH, PW, HC), BF16),
            pltpu.VMEM((NCH, PW, HC), BF16),
            pltpu.VMEM((T, 128), F32),
            pltpu.VMEM((E, T, PWL), BF16),
            pltpu.VMEM((NCH, SLOTS, PW, HC), BF16),
            pltpu.VMEM((E, T, PWL), BF16),
            pltpu.VMEM((PW, E * T), BF16),
            pltpu.VMEM((E, T, 2 * SLOTS * 128), BF16),
            pltpu.VMEM((NCH, E, 2, T, HC), BF16),
            pltpu.VMEM((cfg.RING, SLOTS, E, T, HC), BF16),
            pltpu.VMEM((NCH, SLOTS, PW, HC), BF16),
            pltpu.VMEM((NCH, SLOTS, 2, XR, HC), BF16),
            pltpu.VMEM((NCH, SLOTS - 1, 2, XR, HC), BF16),
            pltpu.VMEM((NCH, SLOTS - 1, 2, XR, HC), BF16),
            pltpu.VMEM((NCH, X, SLOTS, XR, HC), BF16),
            pltpu.VMEM((NCH, 2, XR, HC), BF16),
            pltpu.VMEM((NCH, 2, XR, HC), BF16),
            pltpu.VMEM((NCH, X, XR, HC), BF16),
            pltpu.VMEM((NCH, PW, HC), BF16),
            pltpu.VMEM((E, T, PW), F32),
            pltpu.VMEM((E, T, PWL), BF16),
            pltpu.VMEM((E, T, PWL), BF16),
            *sems(NCH, Y), *sems(NCH, 2), *sems(NCH, Y), *sems(NCH, 2), *sems(E), *sems(E),
            *sems(NCH, SLOTS), *sems(NCH, SLOTS), *sems(NCH, SLOTS), *sems(NCH, SLOTS),
            *sems(NCH, X), *sems(NCH), *sems(NCH, X),
            DMA((2,)), *sems(NCH), *sems(NCH), *sems(NCH),
        ],
        compiler_params=pltpu.CompilerParams(
            collective_id=0, has_side_effects=True, vmem_limit_bytes=63 << 20
        ),
        name="exchange",
    )(
        activations, up_grad, gate_weights.T, route_slot.T, placement.T,
        master[0], moment_one[0], moment_two[0],
    )
    return outs[0], outs[1][None], outs[2][None], outs[3][None]


def solution(mesh, cfg=FULL):
    in_specs = (
        P(("group", "ep"), None),
        P(("group", "ep"), None, None),
        P(("group", "ep"), None),
        P(("group", "ep"), None),
        P(),
        P("group", "ep", None),
        P("group", "ep", None),
        P("group", "ep", None),
    )
    out_specs = (
        P(("group", "ep"), None),
        P("group", "ep", None),
        P("group", "ep", None),
        P("group", "ep", None),
    )
    return jax.shard_map(
        functools.partial(on_device, cfg),
        mesh=mesh, in_specs=in_specs, out_specs=out_specs, check_vma=False,
    )
```

```python
import functools
from types import SimpleNamespace

import jax
import jax.numpy as jnp
from jax import lax
from jax.experimental import pallas as pl
from jax.experimental.pallas import tpu as pltpu
from jax.sharding import PartitionSpec as P

SLOTS = 4
KIND = 4

beta_one = 0.9
beta_two = 0.95
learn_rate = 0.01
decay_rate = 0.1
epsilon = 1e-08
grad_scale = 0.0625

MESH = pl.DeviceIdType.MESH
F32 = jnp.float32
BF16 = jnp.bfloat16

FULL = SimpleNamespace(ZH=2, X=4, Y=4, K=2, T=192, PW=320, NCH=6, HC=256, RING=3, BACK=2, EARLY=2, LAGS=(1, 2, 3, 4, 6, 7))


def kernel(
    cfg, feat, grads, gates, slots, place, master, mom1, mom2,
    ig_out, master_out, mom1_out, mom2_out,
    fv, uv, mv, v1, v2, gm, fs,
    wall, fall, ft, mb, sall, pk, part, ks, rl, rr, x1r, zs, zr, x2s, g2, ba, bs, br,
    ysend, yrecv, hsend, hrecv, csend, crecv, osend, orecv, fsend, frecv, bsend, brecv,
    wrs, wrr, wls, wlr, prs, prr, pls, plr,
    x1ss, x1rs, zss, zrs, x2ss, x2rs,
    lsem, msem, v1sem, v2sem, mosem, o1sem, o2sem,
):
    ZH, X, Y, K, T, PW, NCH, HC = (
        cfg.ZH, cfg.X, cfg.Y, cfg.K, cfg.T, cfg.PW, cfg.NCH, cfg.HC
    )
    E = Y * K
    LAST = SLOTS - 1
    XR = PW // X
    near = {1: (), 2: (1,), 4: (1, 3)}[Y]
    RING, BACK = cfg.RING, cfg.BACK
    g, e = lax.axis_index("group"), lax.axis_index("ep")
    zh, x = g // X, g % X
    z, me = e // E, e % E
    y, k = me // K, me % K

    def plane(peer):
        return (g, z * E + peer)

    def ypeer(dy):
        return ((y + dy) % Y) * K + k

    sib = y * K + (K - 1 - k)
    left, right = (g, e - E), (g, e + E)

    def xpeer(dx):
        return (zh * X + (x + dx) % X, e)

    partner = ((ZH - 1 - zh) * X + x, e)

    def rcopy(src, dst, ss, rs, dev):
        return pltpu.make_async_remote_copy(
            src_ref=src, dst_ref=dst, send_sem=ss, recv_sem=rs, device_id=dev, device_id_type=MESH
        )

    def cols(j):
        return pl.ds(pl.multiple_of(j * HC, HC), HC)

    def load_master(j):
        return pltpu.make_async_copy(master.at[:, cols(j)], mv.at[j], msem.at[j])

    def load_mom1(j):
        return pltpu.make_async_copy(mom1.at[:, cols(j)], v1.at[j], v1sem.at[j])

    def load_mom2(j):
        return pltpu.make_async_copy(mom2.at[:, cols(j)], v2.at[j], v2sem.at[j])

    def store_master(j):
        return pltpu.make_async_copy(mv.at[j], master_out.at[:, cols(j)], mosem.at[j])

    def store_mom1(j):
        return pltpu.make_async_copy(v1.at[j], mom1_out.at[:, cols(j)], o1sem.at[j])

    def store_mom2(j):
        return pltpu.make_async_copy(v2.at[j], mom2_out.at[:, cols(j)], o2sem.at[j])

    load_feat = pltpu.make_async_copy(feat, fv, lsem.at[0])
    load_grads = pltpu.make_async_copy(grads, uv, lsem.at[1])
    load_feat.start()
    load_grads.start()
    for j in range(NCH):
        load_master(j).start()

    barrier = pltpu.get_barrier_semaphore()

    def greet(dev):
        pl.semaphore_signal(barrier, inc=1, device_id=dev, device_id_type=MESH)

    for d in range(1, E):
        greet(plane((me + d) % E))
    for dx in range(1, X):
        greet(xpeer(dx))
    if ZH > 1:
        greet(partner)

    @pl.when(z > 0)
    def _():
        greet(left)

    @pl.when(z < LAST)
    def _():
        greet(right)

    marks = [
        jnp.where(slots[r:r + 1, :] == c, 1.0, 0.0) for c in range(SLOTS) for r in range(2)
    ]
    marks = jnp.concatenate(
        marks + [gates[...], jnp.zeros((128 - 2 * SLOTS - 2, T), F32)], axis=0
    )
    wide = -T % 128
    if wide:
        marks = jnp.concatenate([marks, jnp.zeros((128, wide), F32)], axis=1)
    gm[...] = marks.T[:T]

    PWL = fs.shape[2]
    tail = gm[:, :PWL - PW].astype(BF16)
    load_feat.wait()
    for d in range(E):
        fs[d] = jnp.concatenate([fv[:, d * PW:(d + 1) * PW], tail], axis=1)

    def scale(j):
        for r in range(2):
            gate = gm[:, 2 * SLOTS + r:2 * SLOTS + r + 1]
            sall[j, me, r] = (uv[:, r, cols(j)].astype(F32) * gate).astype(BF16)

    def weights(j):
        load_master(j).wait()
        wall[j, z] = mv[j].astype(BF16)

    pl.semaphore_wait(
        barrier,
        E - 1 + X - 1 + ZH - 1
        + jnp.where(z > 0, 1, 0) + jnp.where(z < LAST, 1, 0),
    )

    def y_copy(j, dy):
        return rcopy(sall.at[j, me], sall.at[j, me], ysend.at[j, dy], yrecv.at[j, dy], plane(ypeer(dy)))

    def y_from(j, dy):
        src = sall.at[j, ypeer(-dy)]
        return rcopy(src, src, ysend.at[j, dy], yrecv.at[j, dy], plane(ypeer(dy)))

    def c_copy(j, dy):
        src = sall.at[j, ypeer(-dy)]
        return rcopy(src, src, csend.at[j, dy], crecv.at[j, dy], plane(sib))

    def c_from(j, dy):
        src = sall.at[j, ((y - dy) % Y) * K + (K - 1 - k)]
        return rcopy(src, src, csend.at[j, dy], crecv.at[j, dy], plane(sib))

    def h_copy(j, dy):
        h = 0 if dy == 1 else 1
        src = sall.at[j, ypeer(-dy), h]
        return rcopy(src, src, hsend.at[j, h], hrecv.at[j, h], plane(ypeer(dy)))

    def h_from(j, h):
        src = sall.at[j, ypeer(2), h]
        return rcopy(src, src, hsend.at[j, h], hrecv.at[j, h], plane(ypeer(1)))

    def o_copy(j, h):
        src = sall.at[j, ypeer(2), h]
        return rcopy(src, src, osend.at[j, h], orecv.at[j, h], plane(sib))

    def o_from(j, h):
        src = sall.at[j, ((y + 2) % Y) * K + (K - 1 - k), h]
        return rcopy(src, src, osend.at[j, h], orecv.at[j, h], plane(sib))

    def f_copy(d):
        peer = (me + d) % E
        return rcopy(fs.at[peer], fall.at[me], fsend.at[d], frecv.at[d], plane(peer))

    def f_from(d):
        src = fall.at[(me - d) % E]
        return rcopy(src, src, fsend.at[d], frecv.at[d], plane((me + d) % E))

    def b_copy(d):
        peer = (me + d) % E
        return rcopy(bs.at[peer], br.at[me], bsend.at[d], brecv.at[d], plane(peer))

    def b_from(d):
        src = br.at[(me - d) % E]
        return rcopy(src, src, bsend.at[d], brecv.at[d], plane((me + d) % E))

    def w_right(j, s, slot):
        return rcopy(wall.at[j, slot], wall.at[j, slot], wrs.at[j, s], wrr.at[j, s], right)

    def w_left(j, s, slot):
        return rcopy(wall.at[j, slot], wall.at[j, slot], wls.at[j, s], wlr.at[j, s], left)

    def w_from_left(j, s, slot):
        return rcopy(wall.at[j, slot], wall.at[j, slot], wrs.at[j, s], wrr.at[j, s], left)

    def w_from_right(j, s, slot):
        return rcopy(wall.at[j, slot], wall.at[j, slot], wls.at[j, s], wlr.at[j, s], right)

    def p_right(j, c):
        return rcopy(ks.at[j, c], rl.at[j, c - 1], prs.at[j, c], prr.at[j, c], right)

    def p_left(j, c):
        return rcopy(ks.at[j, c], rr.at[j, c], pls.at[j, c], plr.at[j, c], left)

    def p_from_left(j, c):
        return rcopy(rl.at[j, c - 1], rl.at[j, c - 1], prs.at[j, c], prr.at[j, c], left)

    def p_from_right(j, c):
        return rcopy(rr.at[j, c], rr.at[j, c], pls.at[j, c], plr.at[j, c], right)

    def xrows(who):
        return pl.ds(pl.multiple_of(who * XR, 16), XR)

    def x1_copy(j, dx):
        return rcopy(
            part.at[j, :, xrows((x + dx) % X)], x1r.at[j, x],
            x1ss.at[j, dx], x1rs.at[j, dx], xpeer(dx),
        )

    def x1_from(j, dx):
        src = x1r.at[j, (x - dx) % X]
        return rcopy(src, src, x1ss.at[j, dx], x1rs.at[j, dx], xpeer(dx))

    def z_copy(j):
        return rcopy(zs.at[j], zr.at[j], zss.at[j], zrs.at[j], partner)

    def x2_copy(j, dx):
        return rcopy(
            x2s.at[j, dx], g2.at[j, xrows(x)], x2ss.at[j, dx], x2rs.at[j, dx], xpeer(dx)
        )

    def x2_from(j, dx):
        src = g2.at[j, xrows((x - dx) % X)]
        return rcopy(src, src, x2ss.at[j, dx], x2rs.at[j, dx], xpeer(dx))

    def send_scaled(j):
        for dy in near:
            y_copy(j, dy).start()
        if K > 1:
            c_copy(j, 0).start()

    def send_weights(j):
        @pl.when(z < LAST)
        def _():
            w_right(j, 0, z).start()

        @pl.when(z > 0)
        def _():
            w_left(j, 0, z).start()

    def pass_weights(j, s):
        zm = LAST - z

        @pl.when(z >= s)
        def _():
            w_from_left(j, s - 1, z - s).wait_recv()

        @pl.when((z >= s) & (z < LAST))
        def _():
            w_right(j, s, z - s).start()

        @pl.when(zm >= s)
        def _():
            w_from_right(j, s - 1, z + s).wait_recv()

        @pl.when((zm >= s) & (z > 0))
        def _():
            w_left(j, s, z + s).start()

    def when_chunk(i, lag, f):
        j = i - lag

        @pl.when((j >= 0) & (j < NCH))
        def _():
            f(j)

    def gather_near(j):
        for dy in near:
            y_from(j, dy).wait_recv()
            if Y == 4:
                h_copy(j, dy).start()
            if K > 1:
                c_copy(j, dy).start()

    def gather_far(j):
        if Y == 4:
            for h in range(2):
                h_from(j, h).wait_recv()
                if K > 1:
                    o_copy(j, h).start()

    def partials(j, ring):
        def pick(b, _):
            for c in range(SLOTS):
                m0 = mb[b, :, (2 * c) * 128:(2 * c + 1) * 128]
                m1 = mb[b, :, (2 * c + 1) * 128:(2 * c + 2) * 128]
                for l in range(HC // 128):
                    ln = slice(l * 128, (l + 1) * 128)
                    pk[ring, c, b, :, ln] = (
                        sall[j, b, 0, :, ln] * m0 + sall[j, b, 1, :, ln] * m1
                    )
            return 0

        lax.fori_loop(0, E, pick, 0)

        def one(c, _):
            part[j, c] = jnp.dot(
                ft[...], pk[ring, c].reshape(E * T, HC), preferred_element_type=F32
            ).astype(BF16)
            return 0

        lax.fori_loop(0, SLOTS, one, 0)

    def kind_of(who, c):
        return jnp.where(place[c, zh * X + who] >= KIND, 1.0, 0.0).astype(F32)

    def kind_sums(j):
        for dx in range(1, X):
            x1_from(j, dx).wait_recv()

        def one(c, _):
            own = part[j, c, xrows(x)].astype(F32)
            weight = kind_of(x, c)
            second = own * weight
            total = own
            for dx in range(1, X):
                who = (x - dx) % X
                got = x1r[j, who, c].astype(F32)
                second += got * kind_of(who, c)
                total += got
            ks[j, c, 0] = (total - second).astype(BF16)
            ks[j, c, 1] = second.astype(BF16)
            return 0

        lax.fori_loop(0, SLOTS, one, 0)

    def reduce_stage(j, s):
        @pl.when(z == s)
        def _():
            for c in range(LAST, s, -1):
                if s > 0:
                    p_from_left(j, c).wait_recv()
                    ks[j, c] = (ks[j, c].astype(F32) + rl[j, c - 1].astype(F32)).astype(BF16)
                p_right(j, c).start()

        @pl.when(z == LAST - s)
        def _():
            for c in range(0, LAST - s):
                if s > 0:
                    p_from_right(j, c).wait_recv()
                    ks[j, c] = (ks[j, c].astype(F32) + rr[j, c].astype(F32)).astype(BF16)
                p_left(j, c).start()

    def finish(j):
        for zz in range(SLOTS):
            @pl.when(z == zz)
            def _(zz=zz):
                total = ks[j, zz].astype(F32)
                if zz > 0:
                    p_from_left(j, zz).wait_recv()
                    total = total + rl[j, zz - 1].astype(F32)
                if zz < LAST:
                    p_from_right(j, zz).wait_recv()
                    total = total + rr[j, zz].astype(F32)
                zs[j] = total.astype(BF16)

        if ZH > 1:
            z_copy(j).start()

    def spread(j):
        zero, one = zs[j, 0].astype(F32), zs[j, 1].astype(F32)
        if ZH > 1:
            z_copy(j).wait_recv()
            zero += zr[j, 0].astype(F32)
            one += zr[j, 1].astype(F32)
        for dx in range(X):
            weight = kind_of((x + dx) % X, z)
            chosen = (one * weight + zero * (1.0 - weight)).astype(BF16)
            if dx == 0:
                g2[j, xrows(x)] = chosen
            else:
                x2s[j, dx] = chosen
                x2_copy(j, dx).start()

    def collect(j):
        for dx in range(1, X):
            x2_from(j, dx).wait_recv()
        load_mom1(j).wait()
        load_mom2(j).wait()

        def update(b, _):
            rows = xrows(b)
            gradient = g2[j, rows].astype(F32) * grad_scale
            first = beta_one * v1[j, rows].astype(F32) + (1.0 - beta_one) * gradient
            second = beta_two * v2[j, rows].astype(F32) + (1.0 - beta_two) * gradient * gradient
            change = (
                first
                / (1.0 - beta_one**10)
                / (jnp.sqrt(second / (1.0 - beta_two**10)) + epsilon)
            )
            old = mv[j, rows]
            mv[j, rows] = old - learn_rate * (change + decay_rate * old)
            v1[j, rows] = first.astype(BF16)
            v2[j, rows] = second.astype(BF16)
            return 0

        lax.fori_loop(0, X, update, 0)
        store_master(j).start()
        store_mom1(j).start()
        store_mom2(j).start()

    def back(j, ring):
        pass_weights(j, 3)

        def block(b, _):
            total = ba[b]
            for c in range(SLOTS):
                total += lax.dot_general(
                    pk[ring, c, b], wall[j, c], (((1,), (1,)), ((), ())),
                    preferred_element_type=F32,
                )
            ba[b] = total
            return 0

        lax.fori_loop(0, E, block, 0)

    for d in range(1, E):
        f_copy(d).start()

    def first_weights(j, _):
        weights(j)
        send_weights(j)
        return 0

    lax.fori_loop(0, NCH, first_weights, 0)
    load_grads.wait()

    def scale_all(j, _):
        scale(j)
        load_mom1(j).start()
        load_mom2(j).start()
        return 0

    lax.fori_loop(0, NCH, scale_all, 0)
    fall[me] = fs[me]

    def clear(b, _):
        ba[b] = jnp.zeros((T, PW), F32)
        return 0

    lax.fori_loop(0, E, clear, 0)
    for j in range(cfg.EARLY):
        pass_weights(j, 1)
    send_scaled(0)
    for d in range(1, E):
        f_from(d).wait_recv()

    first = (PW // 128) * 128
    spot = lax.broadcasted_iota(jnp.int32, (128, 2 * SLOTS * 128), 0)
    lane = lax.broadcasted_iota(jnp.int32, (128, 2 * SLOTS * 128), 1)
    pick_lane = jnp.where(spot - (PW - first) == lane // 128, 1.0, 0.0).astype(BF16)

    def masks(b, _):
        mb[b] = jnp.dot(
            fall[b, :, first:first + 128], pick_lane, preferred_element_type=F32
        ).astype(BF16)
        return 0

    lax.fori_loop(0, E, masks, 0)
    ft[...] = fall[...].reshape(E * T, fall.shape[2]).T[:PW]
    gather_near(0)
    send_scaled(1)
    gather_far(0)
    for j in range(cfg.EARLY, NCH):
        pass_weights(j, 1)

    lags = cfg.LAGS

    def step(i, _):
        when_chunk(i, -2, send_scaled)
        when_chunk(i, -1, gather_near)
        when_chunk(2 * i, 0, lambda j: pass_weights(j, 2))
        when_chunk(2 * i + 1, 0, lambda j: pass_weights(j, 2))

        def sums(j):
            kind_sums(j)
            reduce_stage(j, 0)


        def compute(j):
            if K > 1:
                for dy in (0, *near):
                    c_from(j, dy).wait_recv()
                if Y == 4:
                    for h in range(2):
                        o_from(j, h).wait_recv()
            partials(j, j % RING)
            for dx in range(1, X):
                x1_copy(j, dx).start()

        when_chunk(i, 0, compute)
        when_chunk(i, -1, gather_far)
        when_chunk(i, lags[0], sums)
        when_chunk(i, lags[1], lambda j: reduce_stage(j, 1))
        when_chunk(i, lags[2], lambda j: reduce_stage(j, 2))
        when_chunk(i, lags[3], finish)
        when_chunk(i, lags[4], spread)
        when_chunk(i, lags[5], collect)
        when_chunk(i, BACK, lambda j: back(j, j % RING))

        @pl.when(i == NCH - 1 + BACK)
        def _():
            def out(b, _):
                bs[b, :, :PW] = ba[b].astype(BF16)
                return 0

            lax.fori_loop(0, E, out, 0)
            for d in range(1, E):
                b_copy(d).start()

        return 0

    lax.fori_loop(0, NCH + lags[5], step, 0)

    br[me] = bs[me]
    for d in range(1, E):
        b_from(d).wait_recv()
    for d in range(E):
        ig_out[:, d * PW:(d + 1) * PW] = br[d, :, :PW]

    for d in range(1, E):
        f_copy(d).wait_send()
        b_copy(d).wait_send()

    def drain(j, _):
        for dy in near:
            y_copy(j, dy).wait_send()
            if Y == 4:
                h_copy(j, dy).wait_send()
        if K > 1:
            for dy in (0, *near):
                c_copy(j, dy).wait_send()
            if Y == 4:
                for h in range(2):
                    o_copy(j, h).wait_send()
        for s in range(SLOTS - 1):
            @pl.when((z >= s) & (z < LAST))
            def _(s=s):
                w_right(j, s, z - s).wait_send()

            @pl.when((LAST - z >= s) & (z > 0))
            def _(s=s):
                w_left(j, s, z + s).wait_send()

            @pl.when(z == s)
            def _(s=s):
                for c in range(LAST, s, -1):
                    p_right(j, c).wait_send()

            @pl.when(z == LAST - s)
            def _(s=s):
                for c in range(0, LAST - s):
                    p_left(j, c).wait_send()

        for dx in range(1, X):
            x1_copy(j, dx).wait_send()
            x2_copy(j, dx).wait_send()
        if ZH > 1:
            z_copy(j).wait_send()
        store_master(j).wait()
        store_mom1(j).wait()
        store_mom2(j).wait()
        return 0

    lax.fori_loop(0, NCH, drain, 0)


def hand_out(arrays):
    parts = 4
    count = len(arrays)

    def body(*refs):
        held, load, store = refs[2 * count:3 * count], refs[-2], refs[-1]
        moves = []
        for n in range(count):
            rows = arrays[n].shape[0] // parts
            for p in range(parts):
                cut = pl.ds(p * rows, rows)
                moves.append((
                    pltpu.make_async_copy(refs[n].at[cut], held[n].at[cut], load.at[n, p]),
                    pltpu.make_async_copy(held[n].at[cut], refs[count + n].at[cut], store.at[n, p]),
                ))
        for first, _ in moves:
            first.start()
        for first, second in moves:
            first.wait()
            second.start()
        for _, second in moves:
            second.wait()

    hbm = pl.BlockSpec(memory_space=pl.ANY)
    sems = pltpu.SemaphoreType.DMA((count, parts))
    return pl.pallas_call(
        body,
        out_shape=[jax.ShapeDtypeStruct(a.shape, a.dtype) for a in arrays],
        in_specs=[hbm] * count,
        out_specs=[hbm] * count,
        scratch_shapes=[*[pltpu.VMEM(a.shape, a.dtype) for a in arrays], sems, sems],
        compiler_params=pltpu.CompilerParams(vmem_limit_bytes=63 << 20),
        name="hand_out",
    )(*arrays)


def on_device(
    cfg, activations, up_grad, gate_weights, route_slot, placement, master, moment_one, moment_two
):
    X, Y, K, T, PW, NCH, HC = cfg.X, cfg.Y, cfg.K, cfg.T, cfg.PW, cfg.NCH, cfg.HC
    E = Y * K
    PWL = PW + -PW % 128
    XR = PW // X
    DMA = pltpu.SemaphoreType.DMA
    vm = pl.BlockSpec(memory_space=pltpu.VMEM)
    sm = pl.BlockSpec(memory_space=pltpu.SMEM)
    hbm = pl.BlockSpec(memory_space=pl.ANY)

    def sems(*shape):
        return [DMA(shape), DMA(shape)]

    outs = pl.pallas_call(
        functools.partial(kernel, cfg),
        out_shape=(
            jax.ShapeDtypeStruct((T, E * PW), BF16),
            jax.ShapeDtypeStruct((PW, NCH * HC), F32),
            jax.ShapeDtypeStruct((PW, NCH * HC), BF16),
            jax.ShapeDtypeStruct((PW, NCH * HC), BF16),
        ),
        in_specs=[hbm, hbm, vm, vm, sm, hbm, hbm, hbm],
        out_specs=(vm, hbm, hbm, hbm),
        scratch_shapes=[
            pltpu.VMEM((T, E * PW), BF16),
            pltpu.VMEM((T, 2, NCH * HC), BF16),
            pltpu.VMEM((NCH, PW, HC), F32),
            pltpu.VMEM((NCH, PW, HC), BF16),
            pltpu.VMEM((NCH, PW, HC), BF16),
            pltpu.VMEM((T, 128), F32),
            pltpu.VMEM((E, T, PWL), BF16),
            pltpu.VMEM((NCH, SLOTS, PW, HC), BF16),
            pltpu.VMEM((E, T, PWL), BF16),
            pltpu.VMEM((PW, E * T), BF16),
            pltpu.VMEM((E, T, 2 * SLOTS * 128), BF16),
            pltpu.VMEM((NCH, E, 2, T, HC), BF16),
            pltpu.VMEM((cfg.RING, SLOTS, E, T, HC), BF16),
            pltpu.VMEM((NCH, SLOTS, PW, HC), BF16),
            pltpu.VMEM((NCH, SLOTS, 2, XR, HC), BF16),
            pltpu.VMEM((NCH, SLOTS - 1, 2, XR, HC), BF16),
            pltpu.VMEM((NCH, SLOTS - 1, 2, XR, HC), BF16),
            pltpu.VMEM((NCH, X, SLOTS, XR, HC), BF16),
            pltpu.VMEM((NCH, 2, XR, HC), BF16),
            pltpu.VMEM((NCH, 2, XR, HC), BF16),
            pltpu.VMEM((NCH, X, XR, HC), BF16),
            pltpu.VMEM((NCH, PW, HC), BF16),
            pltpu.VMEM((E, T, PW), F32),
            pltpu.VMEM((E, T, PWL), BF16),
            pltpu.VMEM((E, T, PWL), BF16),
            *sems(NCH, Y), *sems(NCH, 2), *sems(NCH, Y), *sems(NCH, 2), *sems(E), *sems(E),
            *sems(NCH, SLOTS), *sems(NCH, SLOTS), *sems(NCH, SLOTS), *sems(NCH, SLOTS),
            *sems(NCH, X), *sems(NCH), *sems(NCH, X),
            DMA((2,)), *sems(NCH), *sems(NCH), *sems(NCH),
        ],
        compiler_params=pltpu.CompilerParams(
            collective_id=0, has_side_effects=True, vmem_limit_bytes=63 << 20
        ),
        name="exchange",
    )(
        activations, up_grad, gate_weights.T, route_slot.T, placement.T,
        master[0], moment_one[0], moment_two[0],
    )
    outs = hand_out(outs)
    return outs[0], outs[1][None], outs[2][None], outs[3][None]


def solution(mesh, cfg=FULL):
    in_specs = (
        P(("group", "ep"), None),
        P(("group", "ep"), None, None),
        P(("group", "ep"), None),
        P(("group", "ep"), None),
        P(),
        P("group", "ep", None),
        P("group", "ep", None),
        P("group", "ep", None),
    )
    out_specs = (
        P(("group", "ep"), None),
        P("group", "ep", None),
        P("group", "ep", None),
        P("group", "ep", None),
    )
    return jax.shard_map(
        functools.partial(on_device, cfg),
        mesh=mesh, in_specs=in_specs, out_specs=out_specs, check_vma=False,
    )
```

```python
import functools
from types import SimpleNamespace

import jax
import jax.numpy as jnp
from jax import lax
from jax.experimental import pallas as pl
from jax.experimental.pallas import tpu as pltpu
from jax.sharding import PartitionSpec as P

SLOTS = 4
KIND = 4

beta_one = 0.9
beta_two = 0.95
learn_rate = 0.01
decay_rate = 0.1
epsilon = 1e-08
grad_scale = 0.0625

MESH = pl.DeviceIdType.MESH
F32 = jnp.float32
BF16 = jnp.bfloat16

FULL = SimpleNamespace(ZH=2, X=4, Y=4, K=2, T=192, PW=320, NCH=6, HC=256, RING=3, BACK=2, EARLY=2, LAGS=(1, 2, 3, 4, 6, 7))


def kernel(
    cfg, feat, grads, gates, slots, place, master, mom1, mom2,
    ig_out, master_out, mom1_out, mom2_out,
    fv, uv, mv, v1, v2, gm, fs,
    wall, fall, ft, mb, sall, pk, part, ks, rl, rr, x1r, zs, zr, x2s, g2, ba, bs, br,
    ysend, yrecv, hsend, hrecv, csend, crecv, osend, orecv, fsend, frecv, bsend, brecv,
    wrs, wrr, wls, wlr, prs, prr, pls, plr,
    x1ss, x1rs, zss, zrs, x2ss, x2rs,
    lsem, msem, v1sem, v2sem, mosem, o1sem, o2sem,
):
    ZH, X, Y, K, T, PW, NCH, HC = (
        cfg.ZH, cfg.X, cfg.Y, cfg.K, cfg.T, cfg.PW, cfg.NCH, cfg.HC
    )
    E = Y * K
    LAST = SLOTS - 1
    XR = PW // X
    near = {1: (), 2: (1,), 4: (1, 3)}[Y]
    RING, BACK = cfg.RING, cfg.BACK
    g, e = lax.axis_index("group"), lax.axis_index("ep")
    zh, x = g // X, g % X
    z, me = e // E, e % E
    y, k = me // K, me % K

    def plane(peer):
        return (g, z * E + peer)

    def ypeer(dy):
        return ((y + dy) % Y) * K + k

    sib = y * K + (K - 1 - k)
    left, right = (g, e - E), (g, e + E)

    def xpeer(dx):
        return (zh * X + (x + dx) % X, e)

    partner = ((ZH - 1 - zh) * X + x, e)

    def rcopy(src, dst, ss, rs, dev):
        return pltpu.make_async_remote_copy(
            src_ref=src, dst_ref=dst, send_sem=ss, recv_sem=rs, device_id=dev, device_id_type=MESH
        )

    def cols(j):
        return pl.ds(pl.multiple_of(j * HC, HC), HC)

    def load_master(j):
        return pltpu.make_async_copy(master.at[:, cols(j)], mv.at[j], msem.at[j])

    def load_mom1(j):
        return pltpu.make_async_copy(mom1.at[:, cols(j)], v1.at[j], v1sem.at[j])

    def load_mom2(j):
        return pltpu.make_async_copy(mom2.at[:, cols(j)], v2.at[j], v2sem.at[j])

    def store_master(j):
        return pltpu.make_async_copy(mv.at[j], master_out.at[:, cols(j)], mosem.at[j])

    def store_mom1(j):
        return pltpu.make_async_copy(v1.at[j], mom1_out.at[:, cols(j)], o1sem.at[j])

    def store_mom2(j):
        return pltpu.make_async_copy(v2.at[j], mom2_out.at[:, cols(j)], o2sem.at[j])

    load_feat = pltpu.make_async_copy(feat, fv, lsem.at[0])
    load_grads = pltpu.make_async_copy(grads, uv, lsem.at[1])
    load_feat.start()
    load_grads.start()
    for j in range(NCH):
        load_master(j).start()

    barrier = pltpu.get_barrier_semaphore()

    def greet(dev):
        pl.semaphore_signal(barrier, inc=1, device_id=dev, device_id_type=MESH)

    for d in range(1, E):
        greet(plane((me + d) % E))
    for dx in range(1, X):
        greet(xpeer(dx))
    if ZH > 1:
        greet(partner)

    @pl.when(z > 0)
    def _():
        greet(left)

    @pl.when(z < LAST)
    def _():
        greet(right)

    marks = [
        jnp.where(slots[r:r + 1, :] == c, 1.0, 0.0) for c in range(SLOTS) for r in range(2)
    ]
    marks = jnp.concatenate(
        marks + [gates[...], jnp.zeros((128 - 2 * SLOTS - 2, T), F32)], axis=0
    )
    wide = -T % 128
    if wide:
        marks = jnp.concatenate([marks, jnp.zeros((128, wide), F32)], axis=1)
    gm[...] = marks.T[:T]

    PWL = fs.shape[2]
    tail = gm[:, :PWL - PW].astype(BF16)
    load_feat.wait()
    for d in range(E):
        fs[d] = jnp.concatenate([fv[:, d * PW:(d + 1) * PW], tail], axis=1)

    def scale(j):
        for r in range(2):
            gate = gm[:, 2 * SLOTS + r:2 * SLOTS + r + 1]
            sall[j, me, r] = (uv[:, r, cols(j)].astype(F32) * gate).astype(BF16)

    def weights(j):
        load_master(j).wait()
        wall[j, z] = mv[j].astype(BF16)

    pl.semaphore_wait(
        barrier,
        E - 1 + X - 1 + ZH - 1
        + jnp.where(z > 0, 1, 0) + jnp.where(z < LAST, 1, 0),
    )

    def y_copy(j, dy):
        return rcopy(sall.at[j, me], sall.at[j, me], ysend.at[j, dy], yrecv.at[j, dy], plane(ypeer(dy)))

    def y_from(j, dy):
        src = sall.at[j, ypeer(-dy)]
        return rcopy(src, src, ysend.at[j, dy], yrecv.at[j, dy], plane(ypeer(dy)))

    def c_copy(j, dy):
        src = sall.at[j, ypeer(-dy)]
        return rcopy(src, src, csend.at[j, dy], crecv.at[j, dy], plane(sib))

    def c_from(j, dy):
        src = sall.at[j, ((y - dy) % Y) * K + (K - 1 - k)]
        return rcopy(src, src, csend.at[j, dy], crecv.at[j, dy], plane(sib))

    def h_copy(j, dy):
        h = 0 if dy == 1 else 1
        src = sall.at[j, ypeer(-dy), h]
        return rcopy(src, src, hsend.at[j, h], hrecv.at[j, h], plane(ypeer(dy)))

    def h_from(j, h):
        src = sall.at[j, ypeer(2), h]
        return rcopy(src, src, hsend.at[j, h], hrecv.at[j, h], plane(ypeer(1)))

    def o_copy(j, h):
        src = sall.at[j, ypeer(2), h]
        return rcopy(src, src, osend.at[j, h], orecv.at[j, h], plane(sib))

    def o_from(j, h):
        src = sall.at[j, ((y + 2) % Y) * K + (K - 1 - k), h]
        return rcopy(src, src, osend.at[j, h], orecv.at[j, h], plane(sib))

    def f_copy(d):
        peer = (me + d) % E
        return rcopy(fs.at[peer], fall.at[me], fsend.at[d], frecv.at[d], plane(peer))

    def f_from(d):
        src = fall.at[(me - d) % E]
        return rcopy(src, src, fsend.at[d], frecv.at[d], plane((me + d) % E))

    def b_copy(d):
        peer = (me + d) % E
        return rcopy(bs.at[peer], br.at[me], bsend.at[d], brecv.at[d], plane(peer))

    def b_from(d):
        src = br.at[(me - d) % E]
        return rcopy(src, src, bsend.at[d], brecv.at[d], plane((me + d) % E))

    def w_right(j, s, slot):
        return rcopy(wall.at[j, slot], wall.at[j, slot], wrs.at[j, s], wrr.at[j, s], right)

    def w_left(j, s, slot):
        return rcopy(wall.at[j, slot], wall.at[j, slot], wls.at[j, s], wlr.at[j, s], left)

    def w_from_left(j, s, slot):
        return rcopy(wall.at[j, slot], wall.at[j, slot], wrs.at[j, s], wrr.at[j, s], left)

    def w_from_right(j, s, slot):
        return rcopy(wall.at[j, slot], wall.at[j, slot], wls.at[j, s], wlr.at[j, s], right)

    def p_right(j, c):
        return rcopy(ks.at[j, c], rl.at[j, c - 1], prs.at[j, c], prr.at[j, c], right)

    def p_left(j, c):
        return rcopy(ks.at[j, c], rr.at[j, c], pls.at[j, c], plr.at[j, c], left)

    def p_from_left(j, c):
        return rcopy(rl.at[j, c - 1], rl.at[j, c - 1], prs.at[j, c], prr.at[j, c], left)

    def p_from_right(j, c):
        return rcopy(rr.at[j, c], rr.at[j, c], pls.at[j, c], plr.at[j, c], right)

    def xrows(who):
        return pl.ds(pl.multiple_of(who * XR, 16), XR)

    def x1_copy(j, dx):
        return rcopy(
            part.at[j, :, xrows((x + dx) % X)], x1r.at[j, x],
            x1ss.at[j, dx], x1rs.at[j, dx], xpeer(dx),
        )

    def x1_from(j, dx):
        src = x1r.at[j, (x - dx) % X]
        return rcopy(src, src, x1ss.at[j, dx], x1rs.at[j, dx], xpeer(dx))

    def z_copy(j):
        return rcopy(zs.at[j], zr.at[j], zss.at[j], zrs.at[j], partner)

    def x2_copy(j, dx):
        return rcopy(
            x2s.at[j, dx], g2.at[j, xrows(x)], x2ss.at[j, dx], x2rs.at[j, dx], xpeer(dx)
        )

    def x2_from(j, dx):
        src = g2.at[j, xrows((x - dx) % X)]
        return rcopy(src, src, x2ss.at[j, dx], x2rs.at[j, dx], xpeer(dx))

    def send_scaled(j):
        for dy in near:
            y_copy(j, dy).start()
        if K > 1:
            c_copy(j, 0).start()

    def send_weights(j):
        @pl.when(z < LAST)
        def _():
            w_right(j, 0, z).start()

        @pl.when(z > 0)
        def _():
            w_left(j, 0, z).start()

    def pass_weights(j, s):
        zm = LAST - z

        @pl.when(z >= s)
        def _():
            w_from_left(j, s - 1, z - s).wait_recv()

        @pl.when((z >= s) & (z < LAST))
        def _():
            w_right(j, s, z - s).start()

        @pl.when(zm >= s)
        def _():
            w_from_right(j, s - 1, z + s).wait_recv()

        @pl.when((zm >= s) & (z > 0))
        def _():
            w_left(j, s, z + s).start()

    def when_chunk(i, lag, f):
        j = i - lag

        @pl.when((j >= 0) & (j < NCH))
        def _():
            f(j)

    def gather_near(j):
        for dy in near:
            y_from(j, dy).wait_recv()
            if Y == 4:
                h_copy(j, dy).start()
            if K > 1:
                c_copy(j, dy).start()

    def gather_far(j):
        if Y == 4:
            for h in range(2):
                h_from(j, h).wait_recv()
                if K > 1:
                    o_copy(j, h).start()

    def partials(j, ring):
        def pick(b, _):
            for c in range(SLOTS):
                m0 = mb[b, :, (2 * c) * 128:(2 * c + 1) * 128]
                m1 = mb[b, :, (2 * c + 1) * 128:(2 * c + 2) * 128]
                for l in range(HC // 128):
                    ln = slice(l * 128, (l + 1) * 128)
                    pk[ring, c, b, :, ln] = (
                        sall[j, b, 0, :, ln] * m0 + sall[j, b, 1, :, ln] * m1
                    )
            return 0

        lax.fori_loop(0, E, pick, 0)

        def one(c, _):
            part[j, c] = jnp.dot(
                ft[...], pk[ring, c].reshape(E * T, HC), preferred_element_type=F32
            ).astype(BF16)
            return 0

        lax.fori_loop(0, SLOTS, one, 0)

    def kind_of(who, c):
        return jnp.where(place[c, zh * X + who] >= KIND, 1.0, 0.0).astype(F32)

    def kind_sums(j):
        for dx in range(1, X):
            x1_from(j, dx).wait_recv()

        def one(c, _):
            own = part[j, c, xrows(x)].astype(F32)
            weight = kind_of(x, c)
            second = own * weight
            total = own
            for dx in range(1, X):
                who = (x - dx) % X
                got = x1r[j, who, c].astype(F32)
                second += got * kind_of(who, c)
                total += got
            ks[j, c, 0] = (total - second).astype(BF16)
            ks[j, c, 1] = second.astype(BF16)
            return 0

        lax.fori_loop(0, SLOTS, one, 0)

    def reduce_stage(j, s):
        @pl.when(z == s)
        def _():
            for c in range(LAST, s, -1):
                if s > 0:
                    p_from_left(j, c).wait_recv()
                    ks[j, c] = (ks[j, c].astype(F32) + rl[j, c - 1].astype(F32)).astype(BF16)
                p_right(j, c).start()

        @pl.when(z == LAST - s)
        def _():
            for c in range(0, LAST - s):
                if s > 0:
                    p_from_right(j, c).wait_recv()
                    ks[j, c] = (ks[j, c].astype(F32) + rr[j, c].astype(F32)).astype(BF16)
                p_left(j, c).start()

    def finish(j):
        for zz in range(SLOTS):
            @pl.when(z == zz)
            def _(zz=zz):
                total = ks[j, zz].astype(F32)
                if zz > 0:
                    p_from_left(j, zz).wait_recv()
                    total = total + rl[j, zz - 1].astype(F32)
                if zz < LAST:
                    p_from_right(j, zz).wait_recv()
                    total = total + rr[j, zz].astype(F32)
                zs[j] = total.astype(BF16)

        if ZH > 1:
            z_copy(j).start()

    def spread(j):
        zero, one = zs[j, 0].astype(F32), zs[j, 1].astype(F32)
        if ZH > 1:
            z_copy(j).wait_recv()
            zero += zr[j, 0].astype(F32)
            one += zr[j, 1].astype(F32)
        for dx in range(X):
            weight = kind_of((x + dx) % X, z)
            chosen = (one * weight + zero * (1.0 - weight)).astype(BF16)
            if dx == 0:
                g2[j, xrows(x)] = chosen
            else:
                x2s[j, dx] = chosen
                x2_copy(j, dx).start()

    def collect(j):
        for dx in range(1, X):
            x2_from(j, dx).wait_recv()
        load_mom1(j).wait()
        load_mom2(j).wait()

        def update(b, _):
            rows = xrows(b)
            gradient = g2[j, rows].astype(F32) * grad_scale
            first = beta_one * v1[j, rows].astype(F32) + (1.0 - beta_one) * gradient
            second = beta_two * v2[j, rows].astype(F32) + (1.0 - beta_two) * gradient * gradient
            change = (
                first
                / (1.0 - beta_one**10)
                / (jnp.sqrt(second / (1.0 - beta_two**10)) + epsilon)
            )
            old = mv[j, rows]
            mv[j, rows] = old - learn_rate * (change + decay_rate * old)
            v1[j, rows] = first.astype(BF16)
            v2[j, rows] = second.astype(BF16)
            return 0

        lax.fori_loop(0, X, update, 0)
        store_master(j).start()
        store_mom1(j).start()
        store_mom2(j).start()

    def back(j, ring):
        pass_weights(j, 3)

        def block(b, _):
            total = ba[b]
            for c in range(SLOTS):
                total += lax.dot_general(
                    pk[ring, c, b], wall[j, c], (((1,), (1,)), ((), ())),
                    preferred_element_type=F32,
                )
            ba[b] = total
            return 0

        lax.fori_loop(0, E, block, 0)

    for d in range(1, E):
        f_copy(d).start()

    def first_weights(j, _):
        weights(j)
        send_weights(j)
        return 0

    lax.fori_loop(0, NCH, first_weights, 0)
    load_grads.wait()

    def scale_all(j, _):
        scale(j)
        load_mom1(j).start()
        load_mom2(j).start()
        return 0

    lax.fori_loop(0, NCH, scale_all, 0)
    fall[me] = fs[me]

    def clear(b, _):
        ba[b] = jnp.zeros((T, PW), F32)
        return 0

    lax.fori_loop(0, E, clear, 0)
    for j in range(cfg.EARLY):
        pass_weights(j, 1)
    send_scaled(0)
    for d in range(1, E):
        f_from(d).wait_recv()

    first = (PW // 128) * 128
    spot = lax.broadcasted_iota(jnp.int32, (128, 2 * SLOTS * 128), 0)
    lane = lax.broadcasted_iota(jnp.int32, (128, 2 * SLOTS * 128), 1)
    pick_lane = jnp.where(spot - (PW - first) == lane // 128, 1.0, 0.0).astype(BF16)

    def masks(b, _):
        mb[b] = jnp.dot(
            fall[b, :, first:first + 128], pick_lane, preferred_element_type=F32
        ).astype(BF16)
        return 0

    lax.fori_loop(0, E, masks, 0)
    ft[...] = fall[...].reshape(E * T, fall.shape[2]).T[:PW]
    gather_near(0)
    send_scaled(1)
    gather_far(0)
    for j in range(cfg.EARLY, NCH):
        pass_weights(j, 1)

    def drain(j):
        for dy in near:
            y_copy(j, dy).wait_send()
            if Y == 4:
                h_copy(j, dy).wait_send()
        if K > 1:
            for dy in (0, *near):
                c_copy(j, dy).wait_send()
            if Y == 4:
                for h in range(2):
                    o_copy(j, h).wait_send()
        for s in range(SLOTS - 1):
            @pl.when((z >= s) & (z < LAST))
            def _(s=s):
                w_right(j, s, z - s).wait_send()

            @pl.when((LAST - z >= s) & (z > 0))
            def _(s=s):
                w_left(j, s, z + s).wait_send()

            @pl.when(z == s)
            def _(s=s):
                for c in range(LAST, s, -1):
                    p_right(j, c).wait_send()

            @pl.when(z == LAST - s)
            def _(s=s):
                for c in range(0, LAST - s):
                    p_left(j, c).wait_send()

        for dx in range(1, X):
            x1_copy(j, dx).wait_send()
            x2_copy(j, dx).wait_send()
        if ZH > 1:
            z_copy(j).wait_send()

    def assemble():
        br[me] = bs[me]
        for d in range(1, E):
            b_from(d).wait_recv()
        for d in range(E):
            ig_out[:, d * PW:(d + 1) * PW] = br[d, :, :PW]

    lags = cfg.LAGS

    def step(i, _):
        when_chunk(i, -2, send_scaled)
        when_chunk(i, -1, gather_near)
        when_chunk(2 * i, 0, lambda j: pass_weights(j, 2))
        when_chunk(2 * i + 1, 0, lambda j: pass_weights(j, 2))

        def sums(j):
            kind_sums(j)
            reduce_stage(j, 0)


        def compute(j):
            if K > 1:
                for dy in (0, *near):
                    c_from(j, dy).wait_recv()
                if Y == 4:
                    for h in range(2):
                        o_from(j, h).wait_recv()
            partials(j, j % RING)
            for dx in range(1, X):
                x1_copy(j, dx).start()

        when_chunk(i, 0, compute)
        when_chunk(i, -1, gather_far)
        when_chunk(i, lags[0], sums)
        when_chunk(i, lags[1], lambda j: reduce_stage(j, 1))
        when_chunk(i, lags[2], lambda j: reduce_stage(j, 2))
        when_chunk(i, lags[3], finish)
        when_chunk(i, lags[4], spread)
        when_chunk(i, lags[5], drain)

        @pl.when(i == NCH - 1 + lags[5])
        def _():
            assemble()

        when_chunk(i, lags[5], collect)
        when_chunk(i, BACK, lambda j: back(j, j % RING))

        @pl.when(i == NCH - 1 + BACK)
        def _():
            def out(b, _):
                bs[b, :, :PW] = ba[b].astype(BF16)
                return 0

            lax.fori_loop(0, E, out, 0)
            for d in range(1, E):
                b_copy(d).start()

        return 0

    lax.fori_loop(0, NCH + lags[5], step, 0)


    for d in range(1, E):
        f_copy(d).wait_send()
        b_copy(d).wait_send()

    def stored(j, _):
        store_master(j).wait()
        store_mom1(j).wait()
        store_mom2(j).wait()
        return 0

    lax.fori_loop(0, NCH, stored, 0)


def hand_out(arrays):
    parts = 4
    count = len(arrays)

    def body(*refs):
        held, load, store = refs[2 * count:3 * count], refs[-2], refs[-1]
        moves = []
        for n in range(count):
            rows = arrays[n].shape[0] // parts
            for p in range(parts):
                cut = pl.ds(p * rows, rows)
                moves.append((
                    pltpu.make_async_copy(refs[n].at[cut], held[n].at[cut], load.at[n, p]),
                    pltpu.make_async_copy(held[n].at[cut], refs[count + n].at[cut], store.at[n, p]),
                ))
        for first, _ in moves:
            first.start()
        for first, second in moves:
            first.wait()
            second.start()
        for _, second in moves:
            second.wait()

    hbm = pl.BlockSpec(memory_space=pl.ANY)
    sems = pltpu.SemaphoreType.DMA((count, parts))
    return pl.pallas_call(
        body,
        out_shape=[jax.ShapeDtypeStruct(a.shape, a.dtype) for a in arrays],
        in_specs=[hbm] * count,
        out_specs=[hbm] * count,
        scratch_shapes=[*[pltpu.VMEM(a.shape, a.dtype) for a in arrays], sems, sems],
        compiler_params=pltpu.CompilerParams(vmem_limit_bytes=63 << 20),
        name="hand_out",
    )(*arrays)


def on_device(
    cfg, activations, up_grad, gate_weights, route_slot, placement, master, moment_one, moment_two
):
    X, Y, K, T, PW, NCH, HC = cfg.X, cfg.Y, cfg.K, cfg.T, cfg.PW, cfg.NCH, cfg.HC
    E = Y * K
    PWL = PW + -PW % 128
    XR = PW // X
    DMA = pltpu.SemaphoreType.DMA
    vm = pl.BlockSpec(memory_space=pltpu.VMEM)
    sm = pl.BlockSpec(memory_space=pltpu.SMEM)
    hbm = pl.BlockSpec(memory_space=pl.ANY)

    def sems(*shape):
        return [DMA(shape), DMA(shape)]

    outs = pl.pallas_call(
        functools.partial(kernel, cfg),
        out_shape=(
            jax.ShapeDtypeStruct((T, E * PW), BF16),
            jax.ShapeDtypeStruct((PW, NCH * HC), F32),
            jax.ShapeDtypeStruct((PW, NCH * HC), BF16),
            jax.ShapeDtypeStruct((PW, NCH * HC), BF16),
        ),
        in_specs=[hbm, hbm, vm, vm, sm, hbm, hbm, hbm],
        out_specs=(vm, hbm, hbm, hbm),
        scratch_shapes=[
            pltpu.VMEM((T, E * PW), BF16),
            pltpu.VMEM((T, 2, NCH * HC), BF16),
            pltpu.VMEM((NCH, PW, HC), F32),
            pltpu.VMEM((NCH, PW, HC), BF16),
            pltpu.VMEM((NCH, PW, HC), BF16),
            pltpu.VMEM((T, 128), F32),
            pltpu.VMEM((E, T, PWL), BF16),
            pltpu.VMEM((NCH, SLOTS, PW, HC), BF16),
            pltpu.VMEM((E, T, PWL), BF16),
            pltpu.VMEM((PW, E * T), BF16),
            pltpu.VMEM((E, T, 2 * SLOTS * 128), BF16),
            pltpu.VMEM((NCH, E, 2, T, HC), BF16),
            pltpu.VMEM((cfg.RING, SLOTS, E, T, HC), BF16),
            pltpu.VMEM((NCH, SLOTS, PW, HC), BF16),
            pltpu.VMEM((NCH, SLOTS, 2, XR, HC), BF16),
            pltpu.VMEM((NCH, SLOTS - 1, 2, XR, HC), BF16),
            pltpu.VMEM((NCH, SLOTS - 1, 2, XR, HC), BF16),
            pltpu.VMEM((NCH, X, SLOTS, XR, HC), BF16),
            pltpu.VMEM((NCH, 2, XR, HC), BF16),
            pltpu.VMEM((NCH, 2, XR, HC), BF16),
            pltpu.VMEM((NCH, X, XR, HC), BF16),
            pltpu.VMEM((NCH, PW, HC), BF16),
            pltpu.VMEM((E, T, PW), F32),
            pltpu.VMEM((E, T, PWL), BF16),
            pltpu.VMEM((E, T, PWL), BF16),
            *sems(NCH, Y), *sems(NCH, 2), *sems(NCH, Y), *sems(NCH, 2), *sems(E), *sems(E),
            *sems(NCH, SLOTS), *sems(NCH, SLOTS), *sems(NCH, SLOTS), *sems(NCH, SLOTS),
            *sems(NCH, X), *sems(NCH), *sems(NCH, X),
            DMA((2,)), *sems(NCH), *sems(NCH), *sems(NCH),
        ],
        compiler_params=pltpu.CompilerParams(
            collective_id=0, has_side_effects=True, vmem_limit_bytes=63 << 20
        ),
        name="exchange",
    )(
        activations, up_grad, gate_weights.T, route_slot.T, placement.T,
        master[0], moment_one[0], moment_two[0],
    )
    outs = hand_out(outs)
    return outs[0], outs[1][None], outs[2][None], outs[3][None]


def solution(mesh, cfg=FULL):
    in_specs = (
        P(("group", "ep"), None),
        P(("group", "ep"), None, None),
        P(("group", "ep"), None),
        P(("group", "ep"), None),
        P(),
        P("group", "ep", None),
        P("group", "ep", None),
        P("group", "ep", None),
    )
    out_specs = (
        P(("group", "ep"), None),
        P("group", "ep", None),
        P("group", "ep", None),
        P("group", "ep", None),
    )
    return jax.shard_map(
        functools.partial(on_device, cfg),
        mesh=mesh, in_specs=in_specs, out_specs=out_specs, check_vma=False,
    )
```
